512 devices in a mesh: dp: 64 (over y_hi, x, z), tensor: 8 (over y_lo, core).
Axes of the slice: x: 4, y: 8 (y_hi: 2, y_lo: 4; y = y_hi * 4 + y_lo), z: 8, core: 2. Of those that a mesh axis runs over, the one named last changes fastest.
Arguments:
- tokens: bfloat16 [49152, 4096], P(('dp', 'tensor')), may hold values from -6 to 6
- up_cotangent: bfloat16 [49152, 14336], P('dp', 'tensor'), may hold values from -6 to 6
- basis: bfloat16 [4096, 512], P('dp'), may hold values from -0.09375 to 0.09375
- first_moment: float32 [512, 14336], P('dp', 'tensor'), may hold values from -0.001953125 to 0.001953125
- second_moment: float32 [512, 14336], P('dp', 'tensor'), may hold values from 4.0871757e-11 to 4.0871756e-10
Outputs:
- update: float32 [4096, 14336], P('dp', 'tensor')
The draws below stay inside these ranges and needn't reach their ends.
All inputs are finite; a program needn't handle non-finite values.
Results may differ from the reference program's by a relative error of at most 0.0032.
Values may be sent and summed in bfloat16 or wider, within the bound.
A program may use at most 64 MiB of HBM per device.

```python
import math
import jax
import jax.numpy as jnp

D = 4096
FF = 14336
R = 512
TOK_REP = 768
TOKENS = 49152
N_DP = 64


def block_levels(stream_key, extent, split, smallest, largest):
    def one(axis_at, parts):
        heights = jax.random.uniform(jax.random.fold_in(jax.random.fold_in(stream_key, 6), axis_at), (parts,), jnp.float32, smallest / len(split), largest / len(split))
        return jnp.repeat(jnp.exp(heights), extent[axis_at] // parts).reshape((-1,) + (1,) * (len(extent) - axis_at - 1))

    factor_of = one(*split[0])
    for cut in split[1:]:
        factor_of = factor_of * one(*cut)
    return factor_of


def noise(stream_key, shape, scale, bound, split=(), dtype=jnp.bfloat16):
    result = scale * jax.random.normal(stream_key, shape, jnp.float32)
    if split:
        result = result * block_levels(stream_key, shape, split, -0.22, 0.18)
    return jnp.clip(result, -bound, bound).astype(dtype)


def setup_inputs(seed: int = 0) -> dict:
    arg_keys = jax.random.split(jax.random.key(seed), 6)
    return {
        "tokens": noise(arg_keys[0], (TOKENS, D), 1.0, 6.0, ((0, 512),)),
        "up_cotangent": noise(arg_keys[1], (TOKENS, FF), 1.0, 6.0, ((0, 64), (1, 8))),
        "basis": noise(arg_keys[2], (D, R), D ** -0.5, 0.09375, ((0, 64),)),
        "first_moment": noise(arg_keys[3], (R, FF), (R * FF) ** -0.5, 0.001953125, ((0, 64), (1, 8)), jnp.float32),
        "second_moment": jnp.clip(jnp.exp(math.log(4.0871755979665636e-10) - 2.3025851 * jax.random.uniform(arg_keys[4], (R, FF), jnp.float32) ** block_levels(arg_keys[4], (R, FF), ((0, 64), (1, 8)), -0.2, 0.2)), 4.087175736744442e-11, 4.0871755979665636e-10),
    }


def reference(tokens, up_cotangent, basis, first_moment, second_moment):
    projected = jnp.dot(tokens, basis, preferred_element_type=jnp.float32).astype(jnp.bfloat16)
    grad = jnp.dot(projected.T, up_cotangent, preferred_element_type=jnp.float32) / (TOK_REP * N_DP)
    norm = jnp.sqrt(jnp.sum(grad * grad))
    clipped = grad * jnp.minimum(1.0, 1.0 / norm)
    new_first = 0.9 * first_moment + 0.1 * clipped
    new_second = 0.999 * second_moment + 0.001 * clipped * clipped
    first_fix = 1.0 - 0.9 ** 20
    second_fix = 1.0 - 0.999 ** 20
    direction = (new_first / first_fix / (jnp.sqrt(new_second / second_fix) + 1e-08)).astype(jnp.bfloat16)
    return jnp.dot(basis, direction, preferred_element_type=jnp.float32)
```

```python
import functools

import jax
import jax.numpy as jnp
from jax import lax
from jax.experimental import pallas as pl
from jax.experimental.pallas import tpu as pltpu
from jax.sharding import PartitionSpec as P

MESH = pl.DeviceIdType.MESH
NX, NZ, NY = 4, 8, 4
BLK = 8
TOK = 96
FFL = 1792
HALF = FFL // 2
R = 512
RH = R // 2
BROWS = 64
X_ORDER = (0, 1, 3, 2)
Z_ORDER = (0, 1, 7, 2, 6, 3, 5, 4)
ZH = {1: (0, 1, 2, 3), -1: (7, 6, 5, 4)}
XH = {1: (0, 1), -1: (3, 2)}
SIDES = (1, -1)


class Comm:
    def __init__(self, ssem, rsem, coords):
        self.ssem, self.rsem, self.coords = ssem, rsem, coords
        self.n, self.sent, self.ids = 0, [], {}

    def dev(self, yh=None, x=None, z=None, yl=None, c=None):
        own = self.coords
        yh, x, z, yl, c = (o if v is None else v for v, o in zip((yh, x, z, yl, c), own))
        return (yh * 32 + x * 8 + z, yl * 2 + c)

    def slot(self, key):
        if key not in self.ids:
            self.ids[key] = self.n
            self.n += 1
        return self.ids[key]

    def send(self, key, src, dst, dev):
        i = self.slot(key)
        copy = pltpu.make_async_remote_copy(
            src_ref=src, dst_ref=dst, send_sem=self.ssem.at[i], recv_sem=self.rsem.at[i],
            device_id=dev, device_id_type=MESH,
        )
        copy.start()
        self.sent.append(copy)

    def recv(self, key, dst, dev):
        i = self.slot(key)
        pltpu.make_async_remote_copy(
            src_ref=dst, dst_ref=dst, send_sem=self.ssem.at[i], recv_sem=self.rsem.at[i],
            device_id=dev, device_id_type=MESH,
        ).wait_recv()

    def finish(self):
        for copy in self.sent:
            copy.wait_send()
        self.sent = []


def wrap(v, n):
    return lax.rem(v + n, n)


def gather(comm, name, view_a, view_b, start_b):
    _, x, z, _, _ = comm.coords
    for j in range(1, NX):
        comm.send((name, "ax", j), view_a(x, z), view_a(x, z), comm.dev(x=wrap(x + j, NX)))

    def ring_a(s):
        for j in X_ORDER:
            xo = wrap(x - j, NX)
            if s == 1 and j:
                comm.recv((name, "ax", j), view_a(xo, z), comm.dev())
            for side in SIDES:
                zo = wrap(z - side * (s - 1), NZ)
                if s > 1 and (s < 5 or j in XH[side]):
                    comm.recv((name, "az", side, s - 1, j), view_a(xo, zo), comm.dev())
                if s < 4 or (s == 4 and j in XH[side]):
                    comm.send(
                        (name, "az", side, s, j), view_a(xo, zo), view_a(xo, zo), comm.dev(z=wrap(z + side, NZ))
                    )

    def ring_b1(ks):
        for k in ks:
            zo = wrap(z - k, NZ)
            if k:
                comm.recv((name, "bz", k), view_b(x, zo), comm.dev())
            for side in SIDES:
                comm.send((name, "bx", side, 1, k), view_b(x, zo), view_b(x, zo), comm.dev(x=wrap(x + side, NX)))

    def ring_b2(ks):
        for k in ks:
            zo = wrap(z - k, NZ)
            for side in SIDES:
                xo = wrap(x - side, NX)
                comm.recv((name, "bx", side, 1, k), view_b(xo, zo), comm.dev())
                if k in ZH[side]:
                    comm.send(
                        (name, "bx", side, 2, k), view_b(xo, zo), view_b(xo, zo), comm.dev(x=wrap(x + side, NX))
                    )

    start_b()
    for k in Z_ORDER[1:]:
        comm.send((name, "bz", k), view_b(x, z), view_b(x, z), comm.dev(z=wrap(z + k, NZ)))
    ring_a(1)
    ring_b1(Z_ORDER[:3])
    ring_a(2)
    ring_b1(Z_ORDER[3:])
    ring_b2(Z_ORDER[:3])
    ring_a(3)
    ring_b2(Z_ORDER[3:])
    ring_a(4)
    for side in SIDES:
        for k in ZH[side]:
            comm.recv((name, "bx", side, 2, k), view_b(wrap(x - 2 * side, NX), wrap(z - k, NZ)), comm.dev())
    ring_a(5)


def reduce_scatter(comm, block, sa, ra, sb, rb, sax, rax, sbz, rbz):
    _, x, z, _, _ = comm.coords

    def col(side):
        return 0 if side == 1 else 1

    def xa(j):
        return wrap(x + j, NX)

    def zb(k):
        return wrap(z + k, NZ)

    def step_a(s, js, side):
        for j in js:
            value = block(0, xa(j), wrap(z + side * (4 - s), NZ))
            if s >= 2 or (s == 1 and j in XH[side]):
                got = ra.at[col(side), s - 1, j]
                comm.recv(("ra", side, s - 1, j), got, comm.dev())
                value = value + got[...].astype(jnp.float32)
            out = sa.at[col(side), s, j]
            out[...] = value.astype(jnp.bfloat16)
            comm.send(("ra", side, s, j), out, ra.at[col(side), s, j], comm.dev(z=wrap(z + side, NZ)))

    def step_b(s, ks, side):
        for k in ks:
            value = block(1, wrap(x + side * (2 - s), NX), zb(k))
            if s == 1 and k in ZH[side]:
                got = rb.at[col(side), 0, k]
                comm.recv(("rb", side, 0, k), got, comm.dev())
                value = value + got[...].astype(jnp.float32)
            out = sb.at[col(side), s, k]
            out[...] = value.astype(jnp.bfloat16)
            comm.send(("rb", side, s, k), out, rb.at[col(side), s, k], comm.dev(x=wrap(x + side, NX)))

    def last_b(ks):
        for k in ks:
            value = block(1, x, zb(k))
            for side in SIDES:
                got = rb.at[col(side), 1, k]
                comm.recv(("rb", side, 1, k), got, comm.dev())
                value = value + got[...].astype(jnp.float32)
            if k == 0:
                return value
            sbz[k] = value.astype(jnp.bfloat16)
            comm.send(("rbz", k), sbz.at[k], rbz.at[k], comm.dev(z=zb(k)))

    def last_a(js):
        for j in js:
            value = block(0, xa(j), z)
            for side in SIDES:
                got = ra.at[col(side), 3, j]
                comm.recv(("ra", side, 3, j), got, comm.dev())
                value = value + got[...].astype(jnp.float32)
            if j == 0:
                return value
            sax[j] = value.astype(jnp.bfloat16)
            comm.send(("rax", j), sax.at[j], rax.at[j], comm.dev(x=xa(j)))

    for side in SIDES:
        step_a(0, XH[side], side)
        step_b(0, ZH[side][:2], side)
    for side in SIDES:
        step_a(1, XH[-side], side)
        step_b(0, ZH[side][2:], side)
    for i in (0, 1):
        for side in SIDES:
            step_a(1, XH[side][i:i + 1], side)
            step_b(1, ZH[-side][2 * i:2 * i + 2], side)
    for side in SIDES:
        step_a(2, XH[-side], side)
        step_b(1, ZH[side][:2], side)
    for side in SIDES:
        step_a(2, XH[side], side)
        step_b(1, ZH[side][2:], side)
    for side in SIDES:
        step_a(3, XH[-side], side)
    last_b((4, 3, 5))
    for side in SIDES:
        step_a(3, XH[side], side)
    last_b((2, 6, 1, 7))
    last_a((2, 1, 3))
    total_a = last_a((0,))
    total_b = last_b((0,))
    for j in range(1, NX):
        comm.recv(("rax", j), rax.at[j], comm.dev())
        total_a = total_a + rax[j].astype(jnp.float32)
    for k in range(1, NZ):
        comm.recv(("rbz", k), rbz.at[k], comm.dev())
        total_b = total_b + rbz[k].astype(jnp.float32)
    return total_a, total_b


def kernel(
    tok_ref, up_ref, basis_ref, m_ref, v_ref, out_ref,
    toks, upv, bfull, pall, pt, grad, mom, bp,
    sa, ra, sb, rb, sax, rax, sbz, rbz, ys, yr, n1, n2, da, db,
    lsem, ssem, rsem,
):
    d, t = lax.axis_index("dp"), lax.axis_index("tensor")
    yh, x, z, yl, c = lax.div(d, 32), lax.rem(lax.div(d, 8), 4), lax.rem(d, 8), lax.div(t, 2), lax.rem(t, 2)
    comm = Comm(ssem, rsem, (yh, x, z, yl, c))
    other_core = comm.dev(c=1 - c)
    other_run = comm.dev(yh=1 - yh)
    mirror = comm.dev(yh=1 - yh, yl=3 - yl)

    row0 = pl.multiple_of(yh * BLK, BLK)
    up_copy = pltpu.make_async_copy(up_ref, upv, lsem.at[0])
    tok_copy = pltpu.make_async_copy(tok_ref, toks.at[c], lsem.at[1])
    m_copy = pltpu.make_async_copy(m_ref, mom.at[0, pl.ds(row0, BLK)], lsem.at[2])
    v_copy = pltpu.make_async_copy(v_ref, mom.at[1, pl.ds(row0, BLK)], lsem.at[3])
    for copy in (tok_copy, up_copy, m_copy, v_copy):
        copy.start()

    barrier = pltpu.get_barrier_semaphore()
    peers = [other_core, other_run, mirror]
    peers += [comm.dev(x=wrap(x + j, NX)) for j in range(1, NX)]
    peers += [comm.dev(z=wrap(z + k, NZ)) for k in range(1, NZ)]
    peers += [comm.dev(yl=wrap(yl + r, NY)) for r in range(1, NY)]
    for peer in peers:
        pl.semaphore_signal(barrier, inc=1, device_id=peer, device_id_type=MESH)
    bfull[yh, x, z] = basis_ref[:, pl.ds(pl.multiple_of(c * RH, RH), RH)]
    pl.semaphore_wait(barrier, len(peers))

    comm.send("mirror", bfull.at[yh, x, z], bfull.at[yh, x, z], mirror)

    def start_b():
        comm.send("tok", tok_ref, toks.at[c], other_core)
        comm.send("m", m_ref, mom.at[0, pl.ds(row0, BLK)], other_run)
        comm.send("v", v_ref, mom.at[1, pl.ds(row0, BLK)], other_run)
        row = lax.broadcasted_iota(jnp.int32, (R, R), 0)
        column = lax.broadcasted_iota(jnp.int32, (R, R), 1)
        source = ((column >> 3) & 1) * RH + (column >> 4) * BLK + (column & 7)
        pick = jnp.where(row == source, 1.0, 0.0).astype(jnp.bfloat16)
        bp[...] = jnp.dot(basis_ref[...], pick, preferred_element_type=jnp.float32).astype(jnp.bfloat16)
        comm.recv("mirror", bfull.at[1 - yh, x, z], comm.dev())

    gather(
        comm, "basis",
        lambda xo, zo: bfull.at[yh, xo, zo],
        lambda xo, zo: bfull.at[1 - yh, xo, zo],
        start_b,
    )
    tok_copy.wait()
    comm.recv("tok", toks.at[1 - c], comm.dev())

    proj = jnp.zeros((2 * TOK, RH), jnp.float32)
    depth = NZ * BROWS
    for a in range(2):
        for b in range(NX):
            left = toks[:, :, pl.ds((a * NX + b) * depth, depth)].reshape(2 * TOK, depth)
            proj += jnp.dot(left, bfull[a, b].reshape(depth, RH), preferred_element_type=jnp.float32)
    pall[c, yl] = proj.astype(jnp.bfloat16)

    for r in (2, 1, 3):
        comm.send(("p", r), pall.at[c, yl], pall.at[c, yl], comm.dev(yl=wrap(yl + r, NY)))
    comm.send(("q", 0), pall.at[c, yl], pall.at[c, yl], other_core)
    for r in (1, 3, 2):
        piece = pall.at[c, wrap(yl - r, NY)]
        comm.recv(("p", r), piece, comm.dev())
        comm.send(("q", r), piece, piece, other_core)
    up_copy.wait()

    def product(half):
        pt[...] = pall[half].reshape(NY * 2 * TOK, RH).T

        def tile(i, carry):
            columns = pl.ds(pl.multiple_of(i * 256, 256), 256)
            grad[half, :, columns] = jnp.dot(pt[...], upv[:, columns], preferred_element_type=jnp.float32)
            return carry

        lax.fori_loop(0, FFL // 256, tile, 0)

    product(c)
    for r in range(NY):
        comm.recv(("q", r), pall.at[1 - c, wrap(yl - r, NY)], comm.dev())
    product(1 - c)

    def block(half, xo, zo):
        rows = pl.ds(pl.multiple_of((xo * NZ + zo) * BLK, BLK), BLK)
        columns = pl.ds(half * HALF, HALF)
        return jnp.concatenate([grad[0, rows, columns], grad[1, rows, columns]], axis=0)

    total_a, total_b = reduce_scatter(comm, block, sa, ra, sb, rb, sax, rax, sbz, rbz)
    mine = jnp.concatenate([total_a, total_b], axis=1)
    ys[...] = mine.astype(jnp.bfloat16)
    comm.send("yh", ys, yr, other_run)
    comm.recv("yh", yr, comm.dev())
    g = (mine + yr[...].astype(jnp.float32)) * (1.0 / (NY * 2 * TOK * 64))

    sq = jnp.sum(g * g, axis=0, keepdims=True)
    part = sq[:, 0:128]
    for i in range(1, FFL // 128):
        part = part + sq[:, i * 128:(i + 1) * 128]
    n1[0] = part
    for j in range(NX):
        for k in range(NZ):
            if j or k:
                comm.send(
                    ("n1", j, k), n1.at[0], n1.at[j * NZ + k],
                    comm.dev(x=wrap(x + j, NX), z=wrap(z + k, NZ)),
                )
    for j in range(NX):
        for k in range(NZ):
            if j or k:
                comm.recv(("n1", j, k), n1.at[j * NZ + k], comm.dev())
    n2[0] = jnp.sum(n1[...], axis=0)
    for r in range(NY):
        for e in range(2):
            if r or e:
                comm.send(
                    ("n2", r, e), n2.at[0], n2.at[r * 2 + e],
                    comm.dev(yl=wrap(yl + r, NY), c=lax.rem(c + e, 2)),
                )
    m_copy.wait()
    v_copy.wait()
    other_row0 = pl.multiple_of((1 - yh) * BLK, BLK)
    comm.recv("m", mom.at[0, pl.ds(other_row0, BLK)], comm.dev())
    comm.recv("v", mom.at[1, pl.ds(other_row0, BLK)], comm.dev())
    for r in range(NY):
        for e in range(2):
            if r or e:
                comm.recv(("n2", r, e), n2.at[r * 2 + e], comm.dev())
    norm = jnp.sqrt(jnp.sum(jnp.sum(n2[...], axis=0), axis=1, keepdims=True))
    clipped = g * jnp.minimum(1.0, 1.0 / norm)
    new_first = 0.9 * mom[0] + 0.1 * clipped
    new_second = 0.999 * mom[1] + 0.001 * clipped * clipped
    first_fix = 1.0 - 0.9**20
    second_fix = 1.0 - 0.999**20
    direction = (new_first / first_fix / (jnp.sqrt(new_second / second_fix) + 1e-08)).astype(jnp.bfloat16)
    da[x, z] = direction[:, :HALF]
    db[x, z] = direction[:, HALF:]

    gather(
        comm, "direction",
        lambda xo, zo: da.at[xo, zo],
        lambda xo, zo: db.at[xo, zo],
        lambda: None,
    )
    for half, full in enumerate((da, db)):
        out_ref[:, pl.ds(half * HALF, HALF)] = jnp.dot(
            bp[...], full[...].reshape(R, HALF), preferred_element_type=jnp.float32
        )
    comm.finish()


NSEM = 272


def local(tokens, up_cotangent, basis, first_moment, second_moment):
    bf, f32 = jnp.bfloat16, jnp.float32
    any_spec = pl.BlockSpec(memory_space=pl.ANY)
    vmem_spec = pl.BlockSpec(memory_space=pltpu.VMEM)
    return pl.pallas_call(
        kernel,
        out_shape=jax.ShapeDtypeStruct((BROWS, FFL), f32),
        in_specs=[any_spec, any_spec, vmem_spec, any_spec, any_spec],
        out_specs=vmem_spec,
        scratch_shapes=[
            pltpu.VMEM((2, TOK, 4096), bf),
            pltpu.VMEM((NY * 2 * TOK, FFL), bf),
            pltpu.VMEM((2, NX, NZ, BROWS, RH), bf),
            pltpu.VMEM((2, NY, 2 * TOK, RH), bf),
            pltpu.VMEM((RH, NY * 2 * TOK), bf),
            pltpu.VMEM((2, RH, FFL), f32),
            pltpu.VMEM((2, 2 * BLK, FFL), f32),
            pltpu.VMEM((BROWS, R), bf),
            pltpu.VMEM((2, 4, NX, 16, HALF), bf),
            pltpu.VMEM((2, 4, NX, 16, HALF), bf),
            pltpu.VMEM((2, 2, NZ, 16, HALF), bf),
            pltpu.VMEM((2, 2, NZ, 16, HALF), bf),
            pltpu.VMEM((NX, 16, HALF), bf),
            pltpu.VMEM((NX, 16, HALF), bf),
            pltpu.VMEM((NZ, 16, HALF), bf),
            pltpu.VMEM((NZ, 16, HALF), bf),
            pltpu.VMEM((16, FFL), bf),
            pltpu.VMEM((16, FFL), bf),
            pltpu.VMEM((NX * NZ, 1, 128), f32),
            pltpu.VMEM((NY * 2, 1, 128), f32),
            pltpu.VMEM((NX, NZ, 16, HALF), bf),
            pltpu.VMEM((NX, NZ, 16, HALF), bf),
            pltpu.SemaphoreType.DMA((4,)),
            pltpu.SemaphoreType.DMA((NSEM,)),
            pltpu.SemaphoreType.DMA((NSEM,)),
        ],
        compiler_params=pltpu.CompilerParams(
            collective_id=0, has_side_effects=True, vmem_limit_bytes=48 * 2**20
        ),
        cost_estimate=pl.CostEstimate(flops=4 * 10**9, bytes_accessed=2 * 10**7, transcendentals=0),
        name="galore_step",
    )(tokens, up_cotangent, basis, first_moment, second_moment)


def solution(mesh):
    in_specs = (
        P(("dp", "tensor"), None),
        P("dp", "tensor"),
        P("dp", None),
        P("dp", "tensor"),
        P("dp", "tensor"),
    )
    out_specs = P("dp", "tensor")
    return jax.shard_map(local, mesh=mesh, in_specs=in_specs, out_specs=out_specs, check_vma=False)
```

```python
import functools

import jax
import jax.numpy as jnp
from jax import lax
from jax.experimental import pallas as pl
from jax.experimental.pallas import tpu as pltpu
from jax.sharding import PartitionSpec as P

MESH = pl.DeviceIdType.MESH
NX, NZ, NY = 4, 8, 4
BLK = 8
TOK = 96
FFL = 1792
WA, WB = 768, 1024
R = 512
RH = R // 2
RQ = RH // 2
BROWS = 64
X_ORDER = (0, 1, 3, 2)
Z_ORDER = (0, 1, -1, 2, -2, 3, -3, 4)
ZH = {1: (0, 1, 2, 3), -1: (-1, -2, -3, 4)}
XH = {1: (0, 1), -1: (3, 2)}
RZH = {1: (3, 1, 2, 0), -1: (4, -3, -1, -2)}
RXH = {1: (0, 2), -1: (1, 3)}
SIDES = (1, -1)


class Comm:
    def __init__(self, ssem, rsem, coords):
        self.ssem, self.rsem, self.coords = ssem, rsem, coords
        self.n, self.sent, self.ids = 0, [], {}

    def dev(self, yh=None, x=None, z=None, yl=None, c=None):
        own = self.coords
        yh, x, z, yl, c = (o if v is None else v for v, o in zip((yh, x, z, yl, c), own))
        return (yh * 32 + x * 8 + z, yl * 2 + c)

    def slot(self, key):
        if key not in self.ids:
            self.ids[key] = self.n
            self.n += 1
        return self.ids[key]

    def send(self, key, src, dst, dev):
        i = self.slot(key)
        copy = pltpu.make_async_remote_copy(
            src_ref=src, dst_ref=dst, send_sem=self.ssem.at[i], recv_sem=self.rsem.at[i],
            device_id=dev, device_id_type=MESH,
        )
        copy.start()
        self.sent.append(copy)

    def recv(self, key, dst, dev):
        i = self.slot(key)
        pltpu.make_async_remote_copy(
            src_ref=dst, dst_ref=dst, send_sem=self.ssem.at[i], recv_sem=self.rsem.at[i],
            device_id=dev, device_id_type=MESH,
        ).wait_recv()

    def finish(self):
        for copy in self.sent:
            copy.wait_send()
        self.sent = []


def wrap(v, n):
    return lax.rem(v + n, n)


def gather(comm, name, view_a, view_b, start_b):
    _, x, z, _, c = comm.coords
    turn = 1 - 2 * c

    def zs(k):
        return wrap(z + turn * k, NZ)

    def ring_a(s, js):
        for j in js:
            xo = wrap(x - j, NX)
            if s == 1 and j:
                comm.recv((name, "ax", j), view_a(xo, z), comm.dev())
            for side in SIDES:
                zo = wrap(z - side * (s - 1), NZ)
                if s > 1 and (s < 5 or j in XH[side]):
                    comm.recv((name, "az", side, s - 1, j), view_a(xo, zo), comm.dev())
                if s < 4 or (s == 4 and j in XH[side]):
                    comm.send(
                        (name, "az", side, s, j), view_a(xo, zo), view_a(xo, zo), comm.dev(z=wrap(z + side, NZ))
                    )

    def send_b(k, origin, hop):
        comm.send((name, "bz", k), view_b(x, origin), view_b(x, origin), comm.dev(z=zs(hop)))

    def ring_b1(ks):
        for k in ks:
            zo = zs(-k)
            if k:
                comm.recv((name, "bz", k), view_b(x, zo), comm.dev())
            if k == 2:
                send_b(3, zo, 1)
                send_b(4, zo, 2)
            if k == -2:
                send_b(-3, zo, -1)
            for side in SIDES:
                comm.send((name, "bx", side, 1, k), view_b(x, zo), view_b(x, zo), comm.dev(x=wrap(x + side, NX)))

    def ring_b2(ks):
        for k in ks:
            zo = zs(-k)
            for side in SIDES:
                xo = wrap(x - side, NX)
                comm.recv((name, "bx", side, 1, k), view_b(xo, zo), comm.dev())
                if k in ZH[side]:
                    comm.send(
                        (name, "bx", side, 2, k), view_b(xo, zo), view_b(xo, zo), comm.dev(x=wrap(x + side, NX))
                    )

    for j in X_ORDER[1:]:
        comm.send((name, "ax", j), view_a(x, z), view_a(x, z), comm.dev(x=wrap(x + j, NX)))
    ring_a(1, X_ORDER[:1])
    start_b()
    for k in (2, -2, 1, -1):
        send_b(k, z, k)
    ring_b1((0,))
    ring_a(1, X_ORDER[1:])
    ring_a(2, X_ORDER[:1])
    ring_b1((1, -1, 2, -2))
    ring_a(2, X_ORDER[1:])
    ring_b2((0,))
    ring_a(3, X_ORDER[:2])
    ring_b1((3, -3, 4))
    ring_b2((1, -1))
    ring_a(3, X_ORDER[2:])
    ring_b2((2, -2))
    ring_a(4, X_ORDER[:2])
    ring_b2((3, -3))
    ring_a(4, X_ORDER[2:])
    ring_b2((4,))
    ring_a(5, X_ORDER)
    for side in SIDES:
        for k in ZH[side]:
            comm.recv((name, "bx", side, 2, k), view_b(wrap(x - 2 * side, NX), zs(-k)), comm.dev())


class Scatter:
    def __init__(self, comm, block, sa, ra, sb, rb, asum, sax, rax, sbz, rbz):
        self.comm, self.block = comm, block
        self.sa, self.ra, self.sb, self.rb = sa, ra, sb, rb
        self.asum, self.sax, self.rax, self.sbz, self.rbz = asum, sax, rax, sbz, rbz
        _, self.x, self.z, _, c = comm.coords
        self.turn = 1 - 2 * c

    def zs(self, k):
        return wrap(self.z + self.turn * k, NZ)

    def step_a(self, s, js, side):
        comm, n = self.comm, 0 if side == 1 else 1
        for j in js:
            value = self.block(0, j, wrap(self.z + side * (4 - s), NZ))
            if s >= 2 or (s == 1 and j in RXH[side]):
                got = self.ra.at[n, s - 1, j]
                comm.recv(("ra", side, s - 1, j), got, comm.dev())
                value = value + got[...].astype(jnp.float32)
            out = self.sa.at[n, s, j]
            out[...] = value.astype(jnp.bfloat16)
            comm.send(("ra", side, s, j), out, self.ra.at[n, s, j], comm.dev(z=wrap(self.z + side, NZ)))

    def step_b(self, s, ks, side):
        comm, n = self.comm, 0 if side == 1 else 1
        for k in ks:
            value = self.block(1, wrap(self.x + side * (2 - s), NX), self.zs(k))
            if s == 1 and k in RZH[side]:
                got = self.rb.at[n, 0, k % NZ]
                comm.recv(("rb", side, 0, k), got, comm.dev())
                value = value + got[...].astype(jnp.float32)
            out = self.sb.at[n, s, k % NZ]
            out[...] = value.astype(jnp.bfloat16)
            comm.send(("rb", side, s, k), out, self.rb.at[n, s, k % NZ], comm.dev(x=wrap(self.x + side, NX)))

    def last_a(self, js):
        comm = self.comm
        for j in js:
            value = self.block(0, j, self.z)
            for n, side in enumerate(SIDES):
                got = self.ra.at[n, 3, j]
                comm.recv(("ra", side, 3, j), got, comm.dev())
                value = value + got[...].astype(jnp.float32)
            self.asum[j] = value
            self.sax[j] = value.astype(jnp.bfloat16)

    def send_a(self):
        for j in (2, 1, 3):
            xo = wrap(self.x + j, NX)
            self.comm.send(("rax", j), self.sax.at[xo], self.rax.at[j], self.comm.dev(x=xo))

    def total_a(self):
        value = self.asum[self.x]
        for j in (1, 3, 2):
            self.comm.recv(("rax", j), self.rax.at[j], self.comm.dev())
            value = value + self.rax[j].astype(jnp.float32)
        return value

    def got_b(self, k):
        self.comm.recv(("rbz", k), self.rbz.at[k % NZ], self.comm.dev())
        return self.rbz[k % NZ].astype(jnp.float32)

    def last_b(self, ks):
        comm = self.comm
        hop = {3: 1, -3: -1, 4: 2}
        for k in ks:
            value = self.block(1, self.x, self.zs(k))
            for n, side in enumerate(SIDES):
                got = self.rb.at[n, 1, k % NZ]
                comm.recv(("rb", side, 1, k), got, comm.dev())
                value = value + got[...].astype(jnp.float32)
            if k == 2:
                value = value + self.got_b(3) + self.got_b(4)
            if k == -2:
                value = value + self.got_b(-3)
            if k == 0:
                for other in (1, -1, 2, -2):
                    value = value + self.got_b(other)
                return value
            self.sbz[k % NZ] = value.astype(jnp.bfloat16)
            comm.send(("rbz", k), self.sbz.at[k % NZ], self.rbz.at[k % NZ], comm.dev(z=self.zs(hop.get(k, k))))

    def early(self, js):
        for side in SIDES:
            self.step_a(0, [j for j in js if j in RXH[side]], side)
        for side in SIDES:
            self.step_a(1, [j for j in js if j not in RXH[side]], side)

    def rest(self):
        def a(s, js):
            for side in SIDES:
                self.step_a(s, js[side], side)

        first = {1: (0,), -1: (1,)}
        cross = {1: (1,), -1: (0,)}
        first2 = {1: (2,), -1: (3,)}
        cross2 = {1: (3,), -1: (2,)}
        for side in SIDES:
            self.step_b(0, RZH[side][:2], side)
        a(1, first)
        self.early((2, 3))
        for side in SIDES:
            self.step_b(0, RZH[side][2:], side)
        a(2, cross)
        for side in SIDES:
            self.step_b(1, RZH[-side], side)
        a(2, first)
        a(1, first2)
        for side in SIDES:
            self.step_b(1, RZH[side][:2], side)
        a(3, cross)
        a(2, cross2)
        a(3, first)
        for side in SIDES:
            self.step_b(1, RZH[side][2:], side)
        a(2, first2)
        self.last_b((4, 3, -3))
        a(3, cross2)
        self.last_b((1, -1))
        a(3, first2)
        self.last_a((0, 1))
        self.last_b((2, -2))
        self.last_a((2, 3))
        self.send_a()
        value_b = self.last_b((0,))
        value_a = self.total_a()
        return value_a, value_b


def kernel(
    tok_ref, up_ref, basis_ref, m_ref, v_ref, out_ref,
    toks, upv, bas, bfull, pall, pt, grad, mom, bp,
    sa, ra, sb, rb, asum, sax, rax, sbz, rbz, ysa, yra, ysb, yrb, n1, n2, da, db,
    lsem, ssem, rsem,
):
    d, t = lax.axis_index("dp"), lax.axis_index("tensor")
    yh, x, z, yl, c = lax.div(d, 32), lax.rem(lax.div(d, 8), 4), lax.rem(d, 8), lax.div(t, 2), lax.rem(t, 2)
    comm = Comm(ssem, rsem, (yh, x, z, yl, c))
    other_core = comm.dev(c=1 - c)
    other_run = comm.dev(yh=1 - yh)
    mirror = comm.dev(yh=1 - yh, yl=3 - yl)

    half_columns = pl.ds(pl.multiple_of(c * RH, RH), RH)
    b_copy = pltpu.make_async_copy(basis_ref.at[:, half_columns], bfull.at[yh, x, z], lsem.at[0])
    b_copy.start()
    barrier = pltpu.get_barrier_semaphore()
    peers = [other_core, other_run, mirror]
    peers += [comm.dev(x=wrap(x + j, NX)) for j in range(1, NX)]
    peers += [comm.dev(z=wrap(z + k, NZ)) for k in range(1, NZ)]
    peers += [comm.dev(yl=wrap(yl + r, NY)) for r in range(1, NY)]
    for peer in peers:
        pl.semaphore_signal(barrier, inc=1, device_id=peer, device_id_type=MESH)

    row0 = pl.multiple_of(yh * BLK, BLK)
    tok_copy = pltpu.make_async_copy(tok_ref, toks.at[c], lsem.at[1])
    up_copy = pltpu.make_async_copy(up_ref, upv, lsem.at[2])
    m_copy = pltpu.make_async_copy(m_ref, mom.at[0, pl.ds(row0, BLK)], lsem.at[3])
    v_copy = pltpu.make_async_copy(v_ref, mom.at[1, pl.ds(row0, BLK)], lsem.at[4])
    bas_copy = pltpu.make_async_copy(basis_ref, bas, lsem.at[5])
    for copy in (tok_copy, up_copy, m_copy, v_copy, bas_copy):
        copy.start()
    b_copy.wait()
    pl.semaphore_wait(barrier, len(peers))

    comm.send("mirror", bfull.at[yh, x, z], bfull.at[yh, x, z], mirror)

    def start_b():
        comm.send("tok", tok_ref, toks.at[c], other_core)
        comm.send("m", m_ref, mom.at[0, pl.ds(row0, BLK)], other_run)
        comm.send("v", v_ref, mom.at[1, pl.ds(row0, BLK)], other_run)
        comm.recv("mirror", bfull.at[1 - yh, x, z], comm.dev())

    gather(
        comm, "basis",
        lambda xo, zo: bfull.at[yh, xo, zo],
        lambda xo, zo: bfull.at[1 - yh, xo, zo],
        start_b,
    )
    tok_copy.wait()
    comm.recv("tok", toks.at[1 - c], comm.dev())

    proj = jnp.zeros((2 * TOK, RH), jnp.float32)
    depth = NZ * BROWS
    for a in range(2):
        for b in range(NX):
            left = toks[:, :, pl.ds((a * NX + b) * depth, depth)].reshape(2 * TOK, depth)
            proj += jnp.dot(left, bfull[a, b].reshape(depth, RH), preferred_element_type=jnp.float32)
    proj = proj.astype(jnp.bfloat16)

    for q in range(2):
        piece = pall.at[c, q, yl]
        piece[...] = proj[:, q * RQ:(q + 1) * RQ]
        for r in (2, 1, 3):
            comm.send(("p", q, r), piece, piece, comm.dev(yl=wrap(yl + r, NY)))
        comm.send(("q", q, 0), piece, piece, other_core)

    def collect(q):
        for r in (1, 3, 2):
            piece = pall.at[c, q, wrap(yl - r, NY)]
            comm.recv(("p", q, r), piece, comm.dev())
            comm.send(("q", q, r), piece, piece, other_core)
        for r in (0, 1, 3, 2):
            comm.recv(("q", q, r), pall.at[1 - c, q, wrap(yl - r, NY)], comm.dev())

    def product(q):
        for half in range(2):
            pt[half] = pall[half, q].reshape(NY * 2 * TOK, RQ).T

        def tile(i, carry):
            columns = pl.ds(pl.multiple_of(i * 256, 256), 256)
            left = pt[...].reshape(2 * RQ, NY * 2 * TOK)
            value = jnp.dot(left, upv[:, columns], preferred_element_type=jnp.float32)
            for half in range(2):
                grad[half, pl.ds(q * RQ, RQ), columns] = value[half * RQ:(half + 1) * RQ]
            return carry

        lax.fori_loop(0, FFL // 256, tile, 0)

    def block(half, xo, zo):
        rows = pl.ds(pl.multiple_of((xo * NZ + zo) * BLK, BLK), BLK)
        columns = pl.ds(half * WA, WB if half else WA)
        return jnp.concatenate([grad[0, rows, columns], grad[1, rows, columns]], axis=0)

    scatter = Scatter(comm, block, sa, ra, sb, rb, asum, sax, rax, sbz, rbz)
    collect(0)
    up_copy.wait()
    product(0)
    scatter.early((0, 1))
    collect(1)
    product(1)
    total_a, total_b = scatter.rest()
    sums = []
    for name, value, ys, yr in (("ya", total_a, ysa, yra), ("yb", total_b, ysb, yrb)):
        ys[...] = value.astype(jnp.bfloat16)
        comm.send(name, ys, yr, other_run)
    for name, value, yr in (("ya", total_a, yra), ("yb", total_b, yrb)):
        comm.recv(name, yr, comm.dev())
        sums.append(value + yr[...].astype(jnp.float32))
    g = jnp.concatenate(sums, axis=1) * (1.0 / (NY * 2 * TOK * 64))

    sq = jnp.sum(g * g, axis=0, keepdims=True)
    part = sq[:, 0:128]
    for i in range(1, FFL // 128):
        part = part + sq[:, i * 128:(i + 1) * 128]
    n1[0] = part
    for j in range(NX):
        for k in range(NZ):
            if j or k:
                comm.send(
                    ("n1", j, k), n1.at[0], n1.at[j * NZ + k],
                    comm.dev(x=wrap(x + j, NX), z=wrap(z + k, NZ)),
                )
    for j in range(NX):
        for k in range(NZ):
            if j or k:
                comm.recv(("n1", j, k), n1.at[j * NZ + k], comm.dev())
    n2[0] = jnp.sum(n1[...], axis=0)
    for r in range(NY):
        for e in range(2):
            if r or e:
                comm.send(
                    ("n2", r, e), n2.at[0], n2.at[r * 2 + e],
                    comm.dev(yl=wrap(yl + r, NY), c=lax.rem(c + e, 2)),
                )
    bas_copy.wait()
    row = lax.broadcasted_iota(jnp.int32, (R, R), 0)
    column = lax.broadcasted_iota(jnp.int32, (R, R), 1)
    source = ((column >> 3) & 1) * RH + (column >> 4) * BLK + (column & 7)
    pick = jnp.where(row == source, 1.0, 0.0).astype(jnp.bfloat16)
    bp[...] = jnp.dot(bas[...], pick, preferred_element_type=jnp.float32).astype(jnp.bfloat16)
    m_copy.wait()
    v_copy.wait()
    other_row0 = pl.multiple_of((1 - yh) * BLK, BLK)
    comm.recv("m", mom.at[0, pl.ds(other_row0, BLK)], comm.dev())
    comm.recv("v", mom.at[1, pl.ds(other_row0, BLK)], comm.dev())
    for r in range(NY):
        for e in range(2):
            if r or e:
                comm.recv(("n2", r, e), n2.at[r * 2 + e], comm.dev())
    norm = jnp.sqrt(jnp.sum(jnp.sum(n2[...], axis=0), axis=1, keepdims=True))
    clipped = g * jnp.minimum(1.0, 1.0 / norm)
    new_first = 0.9 * mom[0] + 0.1 * clipped
    new_second = 0.999 * mom[1] + 0.001 * clipped * clipped
    first_fix = 1.0 - 0.9**20
    second_fix = 1.0 - 0.999**20
    direction = (new_first / first_fix / (jnp.sqrt(new_second / second_fix) + 1e-08)).astype(jnp.bfloat16)
    da[x, z] = direction[:, :WA]
    db[x, z] = direction[:, WA:]

    gather(
        comm, "direction",
        lambda xo, zo: da.at[xo, zo],
        lambda xo, zo: db.at[xo, zo],
        lambda: None,
    )
    for start, full, width in ((0, da, WA), (WA, db, WB)):
        out_ref[:, pl.ds(start, width)] = jnp.dot(
            bp[...], full[...].reshape(R, width), preferred_element_type=jnp.float32
        )
    comm.finish()


NSEM = 272


def local(tokens, up_cotangent, basis, first_moment, second_moment):
    bf, f32 = jnp.bfloat16, jnp.float32
    hbm_spec = pl.BlockSpec(memory_space=pltpu.HBM)
    vmem_spec = pl.BlockSpec(memory_space=pltpu.VMEM)
    return pl.pallas_call(
        kernel,
        out_shape=jax.ShapeDtypeStruct((BROWS, FFL), f32),
        in_specs=[hbm_spec] * 5,
        out_specs=vmem_spec,
        scratch_shapes=[
            pltpu.VMEM((2, TOK, 4096), bf),
            pltpu.VMEM((NY * 2 * TOK, FFL), bf),
            pltpu.VMEM((BROWS, R), bf),
            pltpu.VMEM((2, NX, NZ, BROWS, RH), bf),
            pltpu.VMEM((2, 2, NY, 2 * TOK, RQ), bf),
            pltpu.VMEM((2, RQ, NY * 2 * TOK), bf),
            pltpu.VMEM((2, RH, FFL), f32),
            pltpu.VMEM((2, 2 * BLK, FFL), f32),
            pltpu.VMEM((BROWS, R), bf),
            pltpu.VMEM((2, 4, NX, 16, WA), bf),
            pltpu.VMEM((2, 4, NX, 16, WA), bf),
            pltpu.VMEM((2, 2, NZ, 16, WB), bf),
            pltpu.VMEM((2, 2, NZ, 16, WB), bf),
            pltpu.VMEM((NX, 16, WA), f32),
            pltpu.VMEM((NX, 16, WA), bf),
            pltpu.VMEM((NX, 16, WA), bf),
            pltpu.VMEM((NZ, 16, WB), bf),
            pltpu.VMEM((NZ, 16, WB), bf),
            pltpu.VMEM((16, WA), bf),
            pltpu.VMEM((16, WA), bf),
            pltpu.VMEM((16, WB), bf),
            pltpu.VMEM((16, WB), bf),
            pltpu.VMEM((NX * NZ, 1, 128), f32),
            pltpu.VMEM((NY * 2, 1, 128), f32),
            pltpu.VMEM((NX, NZ, 16, WA), bf),
            pltpu.VMEM((NX, NZ, 16, WB), bf),
            pltpu.SemaphoreType.DMA((6,)),
            pltpu.SemaphoreType.DMA((NSEM,)),
            pltpu.SemaphoreType.DMA((NSEM,)),
        ],
        compiler_params=pltpu.CompilerParams(
            collective_id=0, has_side_effects=True, vmem_limit_bytes=48 * 2**20
        ),
        cost_estimate=pl.CostEstimate(flops=4 * 10**9, bytes_accessed=2 * 10**7, transcendentals=0),
        name="galore_step",
    )(tokens, up_cotangent, basis, first_moment, second_moment)


def solution(mesh):
    in_specs = (
        P(("dp", "tensor"), None),
        P("dp", "tensor"),
        P("dp", None),
        P("dp", "tensor"),
        P("dp", "tensor"),
    )
    out_specs = P("dp", "tensor")
    return jax.shard_map(local, mesh=mesh, in_specs=in_specs, out_specs=out_specs, check_vma=False)
```

```python
import functools

import jax
import jax.numpy as jnp
from jax import lax
from jax.experimental import pallas as pl
from jax.experimental.pallas import tpu as pltpu
from jax.sharding import PartitionSpec as P

MESH = pl.DeviceIdType.MESH
NX, NZ, NY = 4, 8, 4
BLK = 8
TOK = 96
FFL = 1792
WA, WB = 768, 1024
R = 512
RH = R // 2
RQ = RH // 2
BROWS = 64
X_ORDER = (0, 1, 3, 2)
Z_ORDER = (0, 1, -1, 2, -2, 3, -3, 4)
ZH = {1: (0, 1, 2, 3), -1: (-1, -2, -3, 4)}
XH = {1: (0, 1), -1: (3, 2)}
RZH = {1: (3, 1, 2, 0), -1: (4, -3, -1, -2)}
RXH = {1: (0, 2), -1: (1, 3)}
SIDES = (1, -1)


class Comm:
    def __init__(self, ssem, rsem, coords):
        self.ssem, self.rsem, self.coords = ssem, rsem, coords
        self.n, self.sent, self.ids = 0, [], {}

    def dev(self, yh=None, x=None, z=None, yl=None, c=None):
        own = self.coords
        yh, x, z, yl, c = (o if v is None else v for v, o in zip((yh, x, z, yl, c), own))
        return (yh * 32 + x * 8 + z, yl * 2 + c)

    def slot(self, key):
        if key not in self.ids:
            self.ids[key] = self.n
            self.n += 1
        return self.ids[key]

    def send(self, key, src, dst, dev):
        i = self.slot(key)
        copy = pltpu.make_async_remote_copy(
            src_ref=src, dst_ref=dst, send_sem=self.ssem.at[i], recv_sem=self.rsem.at[i],
            device_id=dev, device_id_type=MESH,
        )
        copy.start()
        self.sent.append(copy)

    def recv(self, key, dst, dev):
        i = self.slot(key)
        pltpu.make_async_remote_copy(
            src_ref=dst, dst_ref=dst, send_sem=self.ssem.at[i], recv_sem=self.rsem.at[i],
            device_id=dev, device_id_type=MESH,
        ).wait_recv()

    def finish(self):
        for copy in self.sent:
            copy.wait_send()
        self.sent = []


def wrap(v, n):
    return lax.rem(v + n, n)


def run(tasks):
    for _, step in sorted(tasks, key=lambda task: task[0]):
        step()


def gather(comm, name, view_a, view_b, begin, begin_b):
    _, x, z, _, c = comm.coords
    turn = 1 - 2 * c

    def zs(k):
        return wrap(z + turn * k, NZ)

    def send_ax():
        for j in X_ORDER[1:]:
            comm.send((name, "ax", j), view_a(x, z), view_a(x, z), comm.dev(x=wrap(x + j, NX)))

    def ring_a(s, js):
        for j in js:
            xo = wrap(x - j, NX)
            if s == 1 and j:
                comm.recv((name, "ax", j), view_a(xo, z), comm.dev())
            for side in SIDES:
                zo = wrap(z - side * (s - 1), NZ)
                if s > 1 and (s < 5 or j in XH[side]):
                    comm.recv((name, "az", side, s - 1, j), view_a(xo, zo), comm.dev())
                if s < 4 or (s == 4 and j in XH[side]):
                    comm.send(
                        (name, "az", side, s, j), view_a(xo, zo), view_a(xo, zo), comm.dev(z=wrap(z + side, NZ))
                    )

    def send_b(k, origin, hop):
        comm.send((name, "bz", k), view_b(x, origin), view_b(x, origin), comm.dev(z=zs(hop)))

    def send_bz():
        for k in (2, -2, 1, -1):
            send_b(k, z, k)

    def ring_b1(ks):
        for k in ks:
            zo = zs(-k)
            if k:
                comm.recv((name, "bz", k), view_b(x, zo), comm.dev())
            if k == 2:
                send_b(3, zo, 1)
                send_b(4, zo, 2)
            if k == -2:
                send_b(-3, zo, -1)
            for side in SIDES:
                comm.send((name, "bx", side, 1, k), view_b(x, zo), view_b(x, zo), comm.dev(x=wrap(x + side, NX)))

    def ring_b2(ks):
        for k in ks:
            zo = zs(-k)
            for side in SIDES:
                xo = wrap(x - side, NX)
                comm.recv((name, "bx", side, 1, k), view_b(xo, zo), comm.dev())
                if k in ZH[side]:
                    comm.send(
                        (name, "bx", side, 2, k), view_b(xo, zo), view_b(xo, zo), comm.dev(x=wrap(x + side, NX))
                    )

    def last_b():
        for side in SIDES:
            for k in ZH[side]:
                comm.recv((name, "bx", side, 2, k), view_b(wrap(x - 2 * side, NX), zs(-k)), comm.dev())

    steps_a = [
        (0.0, send_ax), (0.0, lambda: ring_a(1, (0,))),
        (2.3, lambda: ring_a(2, (0,))), (2.4, lambda: ring_a(1, (1, 3))), (2.9, lambda: ring_a(1, (2,))),
        (4.6, lambda: ring_a(3, (0,))), (4.7, lambda: ring_a(2, (1, 3))), (5.2, lambda: ring_a(2, (2,))),
        (7.0, lambda: ring_a(4, (0,))), (7.2, lambda: ring_a(3, (1, 3))), (7.6, lambda: ring_a(3, (2,))),
        (9.5, lambda: ring_a(4, (1, 3))), (9.9, lambda: ring_a(4, (2,))), (12.3, lambda: ring_a(5, X_ORDER)),
    ]
    steps_b = [
        (0.0, send_bz), (0.0, lambda: ring_b1((0,))),
        (2.3, lambda: ring_b1((1, -1))), (2.4, lambda: ring_b2((0,))), (3.0, lambda: ring_b1((2, -2))),
        (4.7, lambda: ring_b2((1, -1))), (5.4, lambda: ring_b2((2, -2))), (6.0, lambda: ring_b1((3, -3, 4))),
        (8.5, lambda: ring_b2((3, -3, 4))), (10.7, last_b),
    ]
    return [(begin + t, f) for t, f in steps_a] + [(begin_b + t, f) for t, f in steps_b]


class Scatter:
    def __init__(self, comm, name, block, sa, ra, sb, rb, asum, sax, rax, sbz, rbz):
        self.comm, self.name, self.block = comm, name, block
        self.sa, self.ra, self.sb, self.rb = sa, ra, sb, rb
        self.asum, self.sax, self.rax, self.sbz, self.rbz = asum, sax, rax, sbz, rbz
        _, self.x, self.z, _, c = comm.coords
        self.turn = 1 - 2 * c

    def zs(self, k):
        return wrap(self.z + self.turn * k, NZ)

    def step_a(self, s, js, side):
        comm, n = self.comm, 0 if side == 1 else 1
        for j in js:
            value = self.block(0, j, wrap(self.z + side * (4 - s), NZ))
            if s >= 2 or (s == 1 and j in RXH[side]):
                got = self.ra.at[n, s - 1, j]
                comm.recv((self.name, "ra", side, s - 1, j), got, comm.dev())
                value = value + got[...].astype(jnp.float32)
            out = self.sa.at[n, s, j]
            out[...] = value.astype(jnp.bfloat16)
            comm.send((self.name, "ra", side, s, j), out, self.ra.at[n, s, j], comm.dev(z=wrap(self.z + side, NZ)))

    def step_b(self, s, ks, side):
        comm, n = self.comm, 0 if side == 1 else 1
        for k in ks:
            value = self.block(1, wrap(self.x + side * (2 - s), NX), self.zs(k))
            if s == 1 and k in RZH[side]:
                got = self.rb.at[n, 0, k % NZ]
                comm.recv((self.name, "rb", side, 0, k), got, comm.dev())
                value = value + got[...].astype(jnp.float32)
            out = self.sb.at[n, s, k % NZ]
            out[...] = value.astype(jnp.bfloat16)
            comm.send((self.name, "rb", side, s, k), out, self.rb.at[n, s, k % NZ], comm.dev(x=wrap(self.x + side, NX)))

    def last_a(self, js):
        comm = self.comm
        for j in js:
            value = self.block(0, j, self.z)
            for n, side in enumerate(SIDES):
                got = self.ra.at[n, 3, j]
                comm.recv((self.name, "ra", side, 3, j), got, comm.dev())
                value = value + got[...].astype(jnp.float32)
            self.asum[j] = value
            self.sax[j] = value.astype(jnp.bfloat16)

    def send_a(self):
        for j in (2, 1, 3):
            xo = wrap(self.x + j, NX)
            self.comm.send((self.name, "rax", j), self.sax.at[xo], self.rax.at[j], self.comm.dev(x=xo))

    def total_a(self):
        value = self.asum[self.x]
        for j in (1, 3, 2):
            self.comm.recv((self.name, "rax", j), self.rax.at[j], self.comm.dev())
            value = value + self.rax[j].astype(jnp.float32)
        return value

    def got_b(self, k):
        self.comm.recv((self.name, "rbz", k), self.rbz.at[k % NZ], self.comm.dev())
        return self.rbz[k % NZ].astype(jnp.float32)

    def last_b(self, ks):
        comm = self.comm
        hop = {3: 1, -3: -1, 4: 2}
        for k in ks:
            value = self.block(1, self.x, self.zs(k))
            for n, side in enumerate(SIDES):
                got = self.rb.at[n, 1, k % NZ]
                comm.recv((self.name, "rb", side, 1, k), got, comm.dev())
                value = value + got[...].astype(jnp.float32)
            if k == 2:
                value = value + self.got_b(3) + self.got_b(4)
            if k == -2:
                value = value + self.got_b(-3)
            if k == 0:
                for other in (1, -1, 2, -2):
                    value = value + self.got_b(other)
                return value
            self.sbz[k % NZ] = value.astype(jnp.bfloat16)
            comm.send((self.name, "rbz", k), self.sbz.at[k % NZ], self.rbz.at[k % NZ], comm.dev(z=self.zs(hop.get(k, k))))

    def steps(self, begin):
        def a(s, prior):
            for side in SIDES:
                self.step_a(s, RXH[side if prior else -side], side)

        def b(s, prior):
            for side in SIDES:
                self.step_b(s, RZH[side if prior else -side], side)

        steps = [
            (0.0, lambda: a(0, True)), (0.0, lambda: b(0, True)), (0.2, lambda: a(1, False)), (0.3, lambda: b(1, False)),
            (2.3, lambda: a(1, True)), (2.5, lambda: a(2, False)), (2.6, lambda: b(1, True)),
            (4.6, lambda: a(2, True)), (4.9, lambda: a(3, False)),
            (5.2, lambda: self.last_b((4, 3, -3))), (5.8, lambda: self.last_b((1, -1))),
            (7.0, lambda: a(3, True)), (8.5, lambda: self.last_b((2, -2))),
            (9.4, lambda: self.last_a(range(NX))), (9.4, self.send_a),
        ]
        return [(begin + t, f) for t, f in steps]


def kernel(
    tok_ref, up_ref, basis_ref, m_ref, v_ref, out_ref,
    toks, upv, bas, bfull, pall, pt, grad, mom, bp,
    sa, ra, sb, rb, asum, sax, rax, sbz, rbz, ysa, yra, ysb, yrb, gsum, n1, n2, da, db,
    lsem, ssem, rsem,
):
    d, t = lax.axis_index("dp"), lax.axis_index("tensor")
    yh, x, z, yl, c = lax.div(d, 32), lax.rem(lax.div(d, 8), 4), lax.rem(d, 8), lax.div(t, 2), lax.rem(t, 2)
    comm = Comm(ssem, rsem, (yh, x, z, yl, c))
    other_core = comm.dev(c=1 - c)
    other_run = comm.dev(yh=1 - yh)
    mirror = comm.dev(yh=1 - yh, yl=3 - yl)

    b_copies = []
    for q in range(2):
        columns = pl.ds(pl.multiple_of(q * RH + c * RQ, RQ), RQ)
        b_copies.append(pltpu.make_async_copy(basis_ref.at[:, columns], bfull.at[q, yh, x, z], lsem.at[5 + q]))
        b_copies[q].start()
    barrier = pltpu.get_barrier_semaphore()
    peers = [other_core, mirror]
    peers += [comm.dev(x=wrap(x + j, NX)) for j in range(1, NX)]
    peers += [comm.dev(z=wrap(z + k, NZ)) for k in (1, -1, 2, -2)]
    peers += [comm.dev(yl=wrap(yl + r, NY)) for r in range(1, NY)]
    for peer in peers:
        pl.semaphore_signal(barrier, inc=1, device_id=peer, device_id_type=MESH)

    row0 = pl.multiple_of(yh * BLK, BLK)
    tok_copy = pltpu.make_async_copy(tok_ref, toks.at[c], lsem.at[0])
    up_copy = pltpu.make_async_copy(up_ref, upv, lsem.at[1])
    m_copy = pltpu.make_async_copy(m_ref, mom.at[0, pl.ds(row0, BLK)], lsem.at[2])
    v_copy = pltpu.make_async_copy(v_ref, mom.at[1, pl.ds(row0, BLK)], lsem.at[3])
    bas_copy = pltpu.make_async_copy(basis_ref, bas, lsem.at[4])
    for copy in (tok_copy, up_copy, m_copy, v_copy, bas_copy):
        copy.start()
    for copy in b_copies:
        copy.wait()
    pl.semaphore_wait(barrier, len(peers))

    def send_mirror(q):
        comm.send(("mirror", q), bfull.at[q, yh, x, z], bfull.at[q, yh, x, z], mirror)

    def recv_mirror(q):
        comm.recv(("mirror", q), bfull.at[q, 1 - yh, x, z], comm.dev())

    def send_tokens():
        comm.send("tok", tok_ref, toks.at[c], other_core)

    def recv_tokens():
        tok_copy.wait()
        comm.recv("tok", toks.at[1 - c], comm.dev())

    def send_moments():
        comm.send("m", m_ref, mom.at[0, pl.ds(row0, BLK)], other_run)
        comm.send("v", v_ref, mom.at[1, pl.ds(row0, BLK)], other_run)

    def project(q):
        proj = jnp.zeros((2 * TOK, RQ), jnp.float32)
        depth = NZ * BROWS
        for a in range(2):
            for b in range(NX):
                left = toks[:, :, pl.ds((a * NX + b) * depth, depth)].reshape(2 * TOK, depth)
                proj += jnp.dot(left, bfull[q, a, b].reshape(depth, RQ), preferred_element_type=jnp.float32)
        piece = pall.at[q, c, yl]
        piece[...] = proj.astype(jnp.bfloat16)
        for r in (2, 1, 3):
            comm.send(("p", q, r), piece, piece, comm.dev(yl=wrap(yl + r, NY)))
        comm.send(("q", q, 0), piece, piece, other_core)

    def collect(q):
        for r in (1, 3, 2):
            piece = pall.at[q, c, wrap(yl - r, NY)]
            comm.recv(("p", q, r), piece, comm.dev())
            comm.send(("q", q, r), piece, piece, other_core)

    def product(q):
        for r in (0, 1, 3, 2):
            comm.recv(("q", q, r), pall.at[q, 1 - c, wrap(yl - r, NY)], comm.dev())
        for half in range(2):
            pt[half] = pall[q, half].reshape(NY * 2 * TOK, RQ).T

        def tile(i, carry):
            columns = pl.ds(pl.multiple_of(i * 256, 256), 256)
            left = pt[...].reshape(RH, NY * 2 * TOK)
            grad[q, :, columns] = jnp.dot(left, upv[:, columns], preferred_element_type=jnp.float32)
            return carry

        lax.fori_loop(0, FFL // 256, tile, 0)

    def block_of(q):
        def block(half, xo, zo):
            rows = pl.ds(pl.multiple_of((xo * NZ + zo) * BLK, BLK), BLK)
            start, width = (WA, WB // 2) if half else (0, WA // 2)
            parts = [grad[q, rows, pl.ds(start + i * width, width)] for i in range(2)]
            return jnp.concatenate(parts, axis=0)

        return block

    scatters = [
        Scatter(
            comm, ("rs", q), block_of(q),
            *(ref.at[q] for ref in (sa, ra, sb, rb, asum, sax, rax, sbz, rbz)),
        )
        for q in range(2)
    ]
    sums = [[None, None], [None, None]]

    def finish_half(q, half):
        value = scatters[q].last_b((0,)) if half else scatters[q].total_a()
        ys, yr = ((ysa, yra), (ysb, yrb))[half]
        ys[q] = value.astype(jnp.bfloat16)
        comm.send(("y", q, half), ys.at[q], yr.at[q], other_run)
        sums[q][half] = value

    def exchange(q):
        rows = pl.ds(q * BLK, BLK)
        for half, (yr, start, width) in enumerate(((yra, 0, WA // 2), (yrb, WA, WB // 2))):
            comm.recv(("y", q, half), yr.at[q], comm.dev())
            value = (sums[q][half] + yr[q].astype(jnp.float32)) * (1.0 / (NY * 2 * TOK * 64))
            for i in range(2):
                gsum[rows, pl.ds(start + i * width, width)] = value[i * BLK:(i + 1) * BLK]

    tasks = [(0.1, send_tokens), (16.4, recv_tokens), (22.3, up_copy.wait), (27.0, send_moments)]
    for q, late in ((0, 0.0), (1, 5.0)):
        tasks += [
            (0.0, functools.partial(send_mirror, q)),
            (late + 3.8, functools.partial(recv_mirror, q)),
        ]
        tasks += gather(
            comm, ("basis", q),
            lambda xo, zo, q=q: bfull.at[q, yh, xo, zo],
            lambda xo, zo, q=q: bfull.at[q, 1 - yh, xo, zo],
            late, late + 3.9,
        )
        tasks += [
            (late + 16.5, functools.partial(project, q)),
            (late + 21.0, functools.partial(collect, q)),
            (late + 22.4, functools.partial(product, q)),
        ]
        tasks += scatters[q].steps(late + 24.0)
        tasks += [
            (late + 35.5, functools.partial(finish_half, q, 1)),
            (late + 36.5, functools.partial(finish_half, q, 0)),
            (late + 41.5, functools.partial(exchange, q)),
        ]
    run(tasks)
    g = gsum[...]

    sq = jnp.sum(g * g, axis=0, keepdims=True)
    part = sq[:, 0:128]
    for i in range(1, FFL // 128):
        part = part + sq[:, i * 128:(i + 1) * 128]
    n1[0] = part
    for j in range(NX):
        for k in range(NZ):
            if j or k:
                comm.send(
                    ("n1", j, k), n1.at[0], n1.at[j * NZ + k],
                    comm.dev(x=wrap(x + j, NX), z=wrap(z + k, NZ)),
                )
    for j in range(NX):
        for k in range(NZ):
            if j or k:
                comm.recv(("n1", j, k), n1.at[j * NZ + k], comm.dev())
    n2[0] = jnp.sum(n1[...], axis=0)
    for r in range(NY):
        for e in range(2):
            if r or e:
                comm.send(
                    ("n2", r, e), n2.at[0], n2.at[r * 2 + e],
                    comm.dev(yl=wrap(yl + r, NY), c=lax.rem(c + e, 2)),
                )
    bas_copy.wait()
    row = lax.broadcasted_iota(jnp.int32, (R, R), 0)
    column = lax.broadcasted_iota(jnp.int32, (R, R), 1)
    source = ((column >> 3) & 1) * RH + (column >> 4) * BLK + (column & 7)
    pick = jnp.where(row == source, 1.0, 0.0).astype(jnp.bfloat16)
    bp[...] = jnp.dot(bas[...], pick, preferred_element_type=jnp.float32).astype(jnp.bfloat16)
    m_copy.wait()
    v_copy.wait()
    other_row0 = pl.multiple_of((1 - yh) * BLK, BLK)
    comm.recv("m", mom.at[0, pl.ds(other_row0, BLK)], comm.dev())
    comm.recv("v", mom.at[1, pl.ds(other_row0, BLK)], comm.dev())
    for r in range(NY):
        for e in range(2):
            if r or e:
                comm.recv(("n2", r, e), n2.at[r * 2 + e], comm.dev())
    norm = jnp.sqrt(jnp.sum(jnp.sum(n2[...], axis=0), axis=1, keepdims=True))
    clipped = g * jnp.minimum(1.0, 1.0 / norm)
    new_first = 0.9 * mom[0] + 0.1 * clipped
    new_second = 0.999 * mom[1] + 0.001 * clipped * clipped
    first_fix = 1.0 - 0.9**20
    second_fix = 1.0 - 0.999**20
    direction = (new_first / first_fix / (jnp.sqrt(new_second / second_fix) + 1e-08)).astype(jnp.bfloat16)
    da[x, z] = direction[:, :WA]
    db[x, z] = direction[:, WA:]

    run(gather(comm, "direction", lambda xo, zo: da.at[xo, zo], lambda xo, zo: db.at[xo, zo], 0.0, 0.0))
    for start, full, width in ((0, da, WA), (WA, db, WB)):
        out_ref[:, pl.ds(start, width)] = jnp.dot(
            bp[...], full[...].reshape(R, width), preferred_element_type=jnp.float32
        )
    comm.finish()


NSEM = 400


def local(tokens, up_cotangent, basis, first_moment, second_moment):
    bf, f32 = jnp.bfloat16, jnp.float32
    hbm_spec = pl.BlockSpec(memory_space=pltpu.HBM)
    vmem_spec = pl.BlockSpec(memory_space=pltpu.VMEM)
    return pl.pallas_call(
        kernel,
        out_shape=jax.ShapeDtypeStruct((BROWS, FFL), f32),
        in_specs=[hbm_spec] * 5,
        out_specs=vmem_spec,
        scratch_shapes=[
            pltpu.VMEM((2, TOK, 4096), bf),
            pltpu.VMEM((NY * 2 * TOK, FFL), bf),
            pltpu.VMEM((BROWS, R), bf),
            pltpu.VMEM((2, 2, NX, NZ, BROWS, RQ), bf),
            pltpu.VMEM((2, 2, NY, 2 * TOK, RQ), bf),
            pltpu.VMEM((2, RQ, NY * 2 * TOK), bf),
            pltpu.VMEM((2, RH, FFL), f32),
            pltpu.VMEM((2, 2 * BLK, FFL), f32),
            pltpu.VMEM((BROWS, R), bf),
            pltpu.VMEM((2, 2, 4, NX, 16, WA // 2), bf),
            pltpu.VMEM((2, 2, 4, NX, 16, WA // 2), bf),
            pltpu.VMEM((2, 2, 2, NZ, 16, WB // 2), bf),
            pltpu.VMEM((2, 2, 2, NZ, 16, WB // 2), bf),
            pltpu.VMEM((2, NX, 16, WA // 2), f32),
            pltpu.VMEM((2, NX, 16, WA // 2), bf),
            pltpu.VMEM((2, NX, 16, WA // 2), bf),
            pltpu.VMEM((2, NZ, 16, WB // 2), bf),
            pltpu.VMEM((2, NZ, 16, WB // 2), bf),
            pltpu.VMEM((2, 16, WA // 2), bf),
            pltpu.VMEM((2, 16, WA // 2), bf),
            pltpu.VMEM((2, 16, WB // 2), bf),
            pltpu.VMEM((2, 16, WB // 2), bf),
            pltpu.VMEM((2 * BLK, FFL), f32),
            pltpu.VMEM((NX * NZ, 1, 128), f32),
            pltpu.VMEM((NY * 2, 1, 128), f32),
            pltpu.VMEM((NX, NZ, 16, WA), bf),
            pltpu.VMEM((NX, NZ, 16, WB), bf),
            pltpu.SemaphoreType.DMA((7,)),
            pltpu.SemaphoreType.DMA((NSEM,)),
            pltpu.SemaphoreType.DMA((NSEM,)),
        ],
        compiler_params=pltpu.CompilerParams(
            collective_id=0, has_side_effects=True, vmem_limit_bytes=63 * 2**20
        ),
        cost_estimate=pl.CostEstimate(flops=4 * 10**9, bytes_accessed=2 * 10**7, transcendentals=0),
        name="galore_step",
    )(tokens, up_cotangent, basis, first_moment, second_moment)


def solution(mesh):
    in_specs = (
        P(("dp", "tensor"), None),
        P("dp", "tensor"),
        P("dp", None),
        P("dp", "tensor"),
        P("dp", "tensor"),
    )
    out_specs = P("dp", "tensor")
    return jax.shard_map(local, mesh=mesh, in_specs=in_specs, out_specs=out_specs, check_vma=False)
```

```python
import functools

import jax
import jax.numpy as jnp
from jax import lax
from jax.experimental import pallas as pl
from jax.experimental.pallas import tpu as pltpu
from jax.sharding import PartitionSpec as P

MESH = pl.DeviceIdType.MESH
NX, NZ, NY = 4, 8, 4
BLK = 8
TOK = 96
FFL = 1792
WA, WB = 768, 1024
R = 512
RH = R // 2
RQ = RH // 2
BROWS = 64
X_ORDER = (0, 1, 3, 2)
Z_ORDER = (0, 1, -1, 2, -2, 3, -3, 4)
ZH = {1: (0, 1, 2, 3), -1: (-1, -2, -3, 4)}
XH = {1: (0, 1), -1: (3, 2)}
RZH = {1: (3, 1, 2, 0), -1: (4, -3, -1, -2)}
RXH = {1: (0, 2), -1: (1, 3)}
SIDES = (1, -1)


UNIT = 16 * 128 * 2
UNITS = 320


class Comm:
    def __init__(self, ssem, rsem, tally, coords):
        self.ssem, self.rsem, self.tally, self.coords = ssem, rsem, tally, coords
        self.groups, self.phases, self.coming, self.going = {}, {}, {}, {}

    def dev(self, yh=None, x=None, z=None, yl=None, c=None):
        own = self.coords
        yh, x, z, yl, c = (o if v is None else v for v, o in zip((yh, x, z, yl, c), own))
        return (yh * 32 + x * 8 + z, yl * 2 + c)

    def send(self, phase, group, src, dst, dev):
        i = self.phases.setdefault(phase, len(self.phases))
        j = self.groups.setdefault((phase, group), len(self.groups))
        pltpu.make_async_remote_copy(
            src_ref=src, dst_ref=dst, send_sem=self.ssem.at[i], recv_sem=self.rsem.at[j],
            device_id=dev, device_id_type=MESH,
        ).start()
        size = src.dtype.itemsize
        for n in src.shape:
            size *= n
        self.going[phase] = self.going.get(phase, 0) + size
        self.coming[phase, group] = self.coming.get((phase, group), 0) + size

    def total(self, size, ref):
        if ref is None:
            assert size % UNIT == 0 and size <= UNIT * UNITS
            ref = self.tally.at[pl.ds(0, size // UNIT)]
        return ref

    def wait(self, phase, group, ref=None):
        ref = self.total(self.coming.pop((phase, group)), ref)
        j = self.groups[phase, group]
        pltpu.make_async_remote_copy(
            src_ref=ref, dst_ref=ref, send_sem=self.ssem.at[0], recv_sem=self.rsem.at[j],
            device_id=self.dev(), device_id_type=MESH,
        ).wait_recv()

    def sent(self, phase, ref=None):
        ref = self.total(self.going.pop(phase), ref)
        pltpu.make_async_remote_copy(
            src_ref=ref, dst_ref=ref, send_sem=self.ssem.at[self.phases[phase]], recv_sem=self.rsem.at[0],
            device_id=self.dev(), device_id_type=MESH,
        ).wait_send()

    def finish(self):
        for phase in list(self.going):
            self.sent(phase)


def wrap(v, n):
    return lax.rem(v + n, n)


def run(tasks):
    for _, step in sorted(tasks, key=lambda task: task[0]):
        step()


def gather(comm, name, view_a, view_b, begin, begin_b):
    _, x, z, _, c = comm.coords
    turn = 1 - 2 * c

    def zs(k):
        return wrap(z + turn * k, NZ)

    near = {0: 0, 1: 1, 3: 1, 2: 2}
    far = {0: 0, 1: 1, -1: 1, 2: 2, -2: 2, 3: 3, -3: 3, 4: 3}
    name_a, name_b = (name, "a"), (name, "b")

    def send_ax():
        for j in X_ORDER[1:]:
            comm.send(name_a, ("x", near[j]), view_a(x, z), view_a(x, z), comm.dev(x=wrap(x + j, NX)))

    def ring_a(s, js):
        if s == 1 and js[0]:
            comm.wait(name_a, ("x", near[js[0]]))
        if 1 < s < 5:
            comm.wait(name_a, ("z", s - 1, near[js[0]]))
        if s == 5:
            comm.wait(name_a, ("z", 4))
            return
        for j in js:
            xo = wrap(x - j, NX)
            for side in SIDES:
                zo = wrap(z - side * (s - 1), NZ)
                if s < 4 or j in XH[side]:
                    group = ("z", s, near[j]) if s < 4 else ("z", 4)
                    comm.send(name_a, group, view_a(xo, zo), view_a(xo, zo), comm.dev(z=wrap(z + side, NZ)))

    def send_b(k, origin, hop):
        comm.send(name_b, ("z", far[k]), view_b(x, origin), view_b(x, origin), comm.dev(z=zs(hop)))

    def send_bz():
        for k in (2, -2, 1, -1):
            send_b(k, z, k)

    def ring_b1(ks):
        if ks[0]:
            comm.wait(name_b, ("z", far[ks[0]]))
        for k in ks:
            zo = zs(-k)
            if k == 2:
                send_b(3, zo, 1)
                send_b(4, zo, 2)
            if k == -2:
                send_b(-3, zo, -1)
            for side in SIDES:
                comm.send(name_b, ("x", far[k]), view_b(x, zo), view_b(x, zo), comm.dev(x=wrap(x + side, NX)))

    def ring_b2(ks):
        comm.wait(name_b, ("x", far[ks[0]]))
        for k in ks:
            zo = zs(-k)
            for side in SIDES:
                xo = wrap(x - side, NX)
                if k in ZH[side]:
                    comm.send(name_b, "x2", view_b(xo, zo), view_b(xo, zo), comm.dev(x=wrap(x + side, NX)))

    def last_b():
        comm.wait(name_b, "x2")

    steps_a = [
        (0.0, send_ax), (0.0, lambda: ring_a(1, (0,))),
        (2.3, lambda: ring_a(2, (0,))), (2.4, lambda: ring_a(1, (1, 3))), (2.9, lambda: ring_a(1, (2,))),
        (4.6, lambda: ring_a(3, (0,))), (4.7, lambda: ring_a(2, (1, 3))), (5.2, lambda: ring_a(2, (2,))),
        (7.0, lambda: ring_a(4, (0,))), (7.2, lambda: ring_a(3, (1, 3))), (7.6, lambda: ring_a(3, (2,))),
        (9.5, lambda: ring_a(4, (1, 3))), (9.9, lambda: ring_a(4, (2,))), (12.3, lambda: ring_a(5, X_ORDER)),
    ]
    steps_b = [
        (0.0, send_bz), (0.0, lambda: ring_b1((0,))),
        (2.3, lambda: ring_b1((1, -1))), (2.4, lambda: ring_b2((0,))), (3.0, lambda: ring_b1((2, -2))),
        (4.7, lambda: ring_b2((1, -1))), (5.4, lambda: ring_b2((2, -2))), (6.0, lambda: ring_b1((3, -3, 4))),
        (8.5, lambda: ring_b2((3, -3, 4))), (10.7, last_b),
    ]
    return [(begin + t, f) for t, f in steps_a] + [(begin_b + t, f) for t, f in steps_b]


class Scatter:
    def __init__(self, comm, name, block, sa, ra, sb, rb, asum, sax, rax, sbz, rbz):
        self.comm, self.name_a, self.name_b, self.block = comm, (name, "a"), (name, "b"), block
        self.last = {0: 0, 1: 1, -1: 1, 2: 2, -2: 2, 3: 3, -3: 3, 4: 3}
        self.sa, self.ra, self.sb, self.rb = sa, ra, sb, rb
        self.asum, self.sax, self.rax, self.sbz, self.rbz = asum, sax, rax, sbz, rbz
        _, self.x, self.z, _, c = comm.coords
        self.turn = 1 - 2 * c

    def zs(self, k):
        return wrap(self.z + self.turn * k, NZ)

    def step_a(self, s, prior):
        comm = self.comm
        if s >= 2 or prior and s:
            comm.wait(self.name_a, (s - 1, prior))
        for n, side in enumerate(SIDES):
            for j in RXH[side if prior else -side]:
                value = self.block(0, j, wrap(self.z + side * (4 - s), NZ))
                if s >= 2 or prior and s:
                    value = value + self.ra[n, s - 1, j].astype(jnp.float32)
                out = self.sa.at[n, s, j]
                out[...] = value.astype(jnp.bfloat16)
                group = (s, prior) if s < 3 else 3
                comm.send(self.name_a, group, out, self.ra.at[n, s, j], comm.dev(z=wrap(self.z + side, NZ)))

    def step_b(self, s, prior, part):
        comm = self.comm
        if s and prior:
            comm.wait(self.name_b, (0, part))
        for n, side in enumerate(SIDES):
            for k in RZH[side if prior else -side][2 * part:2 * part + 2]:
                value = self.block(1, wrap(self.x + side * (2 - s), NX), self.zs(k))
                if s and prior:
                    value = value + self.rb[n, 0, k % NZ].astype(jnp.float32)
                out = self.sb.at[n, s, k % NZ]
                out[...] = value.astype(jnp.bfloat16)
                group = (1, self.last[k]) if s else (0, part)
                comm.send(self.name_b, group, out, self.rb.at[n, s, k % NZ], comm.dev(x=wrap(self.x + side, NX)))

    def last_a(self):
        comm = self.comm
        comm.wait(self.name_a, 3)
        for j in range(NX):
            value = self.block(0, j, self.z)
            for n in range(2):
                value = value + self.ra[n, 3, j].astype(jnp.float32)
            self.asum[j] = value
            self.sax[j] = value.astype(jnp.bfloat16)
        for j in (2, 1, 3):
            xo = wrap(self.x + j, NX)
            comm.send(self.name_a, "x", self.sax.at[xo], self.rax.at[j], comm.dev(x=xo))

    def total_a(self):
        value = self.asum[self.x]
        self.comm.wait(self.name_a, "x")
        for j in (1, 3, 2):
            value = value + self.rax[j].astype(jnp.float32)
        return value

    def last_b(self, ks):
        comm = self.comm
        hop = {3: 1, -3: -1, 4: 2}
        plus = {2: (3, 4), -2: (-3,), 0: (1, -1, 2, -2)}
        comm.wait(self.name_b, (1, self.last[ks[0]]))
        if ks[0] in (0, 2):
            comm.wait(self.name_b, ("z", ks[0]))
        for k in ks:
            value = self.block(1, self.x, self.zs(k))
            for n in range(2):
                value = value + self.rb[n, 1, k % NZ].astype(jnp.float32)
            for other in plus.get(k, ()):
                value = value + self.rbz[other % NZ].astype(jnp.float32)
            if k == 0:
                return value
            self.sbz[k % NZ] = value.astype(jnp.bfloat16)
            comm.send(
                self.name_b, ("z", 2 if k in hop else 0), self.sbz.at[k % NZ], self.rbz.at[k % NZ],
                comm.dev(z=self.zs(hop.get(k, k))),
            )

    def steps(self, begin):
        a, b = self.step_a, self.step_b
        steps = [
            (0.0, lambda: a(0, True)), (0.0, lambda: b(0, True, 0)), (0.1, lambda: b(0, True, 1)),
            (0.2, lambda: a(1, False)), (0.3, lambda: b(1, False, 0)), (0.3, lambda: b(1, False, 1)),
            (2.3, lambda: a(1, True)), (2.5, lambda: a(2, False)),
            (2.6, lambda: b(1, True, 0)), (2.9, lambda: b(1, True, 1)),
            (4.6, lambda: a(2, True)), (4.9, lambda: a(3, False)),
            (5.2, lambda: self.last_b((4, 3, -3))), (5.8, lambda: self.last_b((1, -1))),
            (7.0, lambda: a(3, True)), (8.5, lambda: self.last_b((2, -2))), (9.4, self.last_a),
        ]
        return [(begin + t, f) for t, f in steps]


def kernel(
    tok_ref, up_ref, basis_ref, m_ref, v_ref, out_ref,
    toks, upv, bas, bfull, pall, pt, grad, mom, bp,
    sa, ra, sb, rb, asum, sax, rax, sbz, rbz, ysa, yra, ysb, yrb, gsum, n1, n2, da, db,
    tally, lsem, ssem, rsem,
):
    d, t = lax.axis_index("dp"), lax.axis_index("tensor")
    yh, x, z, yl, c = lax.div(d, 32), lax.rem(lax.div(d, 8), 4), lax.rem(d, 8), lax.div(t, 2), lax.rem(t, 2)
    comm = Comm(ssem, rsem, tally, (yh, x, z, yl, c))
    other_core = comm.dev(c=1 - c)
    other_run = comm.dev(yh=1 - yh)
    mirror = comm.dev(yh=1 - yh, yl=3 - yl)

    b_copies = []
    for q in range(2):
        columns = pl.ds(pl.multiple_of(q * RH + c * RQ, RQ), RQ)
        b_copies.append(pltpu.make_async_copy(basis_ref.at[:, columns], bfull.at[q, yh, x, z], lsem.at[5 + q]))
        b_copies[q].start()
    barrier = pltpu.get_barrier_semaphore()
    peers = [other_core, mirror]
    peers += [comm.dev(x=wrap(x + j, NX)) for j in range(1, NX)]
    peers += [comm.dev(z=wrap(z + k, NZ)) for k in (1, -1, 2, -2)]
    peers += [comm.dev(yl=wrap(yl + r, NY)) for r in range(1, NY)]
    for peer in peers:
        pl.semaphore_signal(barrier, inc=1, device_id=peer, device_id_type=MESH)

    row0 = pl.multiple_of(yh * BLK, BLK)
    tok_copy = pltpu.make_async_copy(tok_ref, toks.at[c], lsem.at[0])
    up_copy = pltpu.make_async_copy(up_ref, upv, lsem.at[1])
    m_copy = pltpu.make_async_copy(m_ref, mom.at[0, pl.ds(row0, BLK)], lsem.at[2])
    v_copy = pltpu.make_async_copy(v_ref, mom.at[1, pl.ds(row0, BLK)], lsem.at[3])
    bas_copy = pltpu.make_async_copy(basis_ref, bas, lsem.at[4])
    for copy in b_copies:
        copy.wait()
    pl.semaphore_wait(barrier, len(peers))

    def send_mirror(q):
        comm.send("mirror", q, bfull.at[q, yh, x, z], bfull.at[q, yh, x, z], mirror)

    def recv_mirror(q):
        comm.wait("mirror", q)

    def load_rest():
        for copy in (up_copy, m_copy, v_copy, bas_copy):
            copy.start()

    def send_tokens():
        tok_copy.start()
        comm.send("tok", 0, tok_ref, toks.at[c], other_core)

    def recv_tokens():
        tok_copy.wait()
        comm.wait("tok", 0)

    def send_moments():
        comm.send("moments", 0, m_ref, mom.at[0, pl.ds(row0, BLK)], other_run)
        comm.send("moments", 0, v_ref, mom.at[1, pl.ds(row0, BLK)], other_run)

    def project(q):
        proj = jnp.zeros((2 * TOK, RQ), jnp.float32)
        depth = NZ * BROWS
        for a in range(2):
            for b in range(NX):
                left = toks[:, :, pl.ds((a * NX + b) * depth, depth)].reshape(2 * TOK, depth)
                proj += jnp.dot(left, bfull[q, a, b].reshape(depth, RQ), preferred_element_type=jnp.float32)
        piece = pall.at[q, c, yl]
        piece[...] = proj.astype(jnp.bfloat16)
        for r in (2, 1, 3):
            comm.send("p", (q, r % 2), piece, piece, comm.dev(yl=wrap(yl + r, NY)))
        comm.send("core", q, piece, piece, other_core)

    def collect(q):
        for r in (1, 3, 2):
            piece = pall.at[q, c, wrap(yl - r, NY)]
            if r != 3:
                comm.wait("p", (q, r % 2))
            comm.send("core", q, piece, piece, other_core)

    def product(q):
        comm.wait("core", q)
        for half in range(2):
            pt[half] = pall[q, half].reshape(NY * 2 * TOK, RQ).T

        def tile(i, carry):
            columns = pl.ds(pl.multiple_of(i * 256, 256), 256)
            left = pt[...].reshape(RH, NY * 2 * TOK)
            grad[q, :, columns] = jnp.dot(left, upv[:, columns], preferred_element_type=jnp.float32)
            return carry

        lax.fori_loop(0, FFL // 256, tile, 0)

    def block_of(q):
        def block(half, xo, zo):
            rows = pl.ds(pl.multiple_of((xo * NZ + zo) * BLK, BLK), BLK)
            start, width = (WA, WB // 2) if half else (0, WA // 2)
            parts = [grad[q, rows, pl.ds(start + i * width, width)] for i in range(2)]
            return jnp.concatenate(parts, axis=0)

        return block

    scatters = [
        Scatter(
            comm, ("rs", q), block_of(q),
            *(ref.at[q] for ref in (sa, ra, sb, rb, asum, sax, rax, sbz, rbz)),
        )
        for q in range(2)
    ]
    sums = [[None, None], [None, None]]

    def finish_half(q, half):
        value = scatters[q].last_b((0,)) if half else scatters[q].total_a()
        ys, yr = ((ysa, yra), (ysb, yrb))[half]
        ys[q] = value.astype(jnp.bfloat16)
        comm.send("y", (q, half), ys.at[q], yr.at[q], other_run)
        sums[q][half] = value

    def exchange(q):
        rows = pl.ds(q * BLK, BLK)
        for half, (yr, start, width) in enumerate(((yra, 0, WA // 2), (yrb, WA, WB // 2))):
            comm.wait("y", (q, half))
            value = (sums[q][half] + yr[q].astype(jnp.float32)) * (1.0 / (NY * 2 * TOK * 64))
            for i in range(2):
                gsum[rows, pl.ds(start + i * width, width)] = value[i * BLK:(i + 1) * BLK]

    tasks = [(2.0, send_tokens), (7.0, load_rest), (16.4, recv_tokens), (22.3, up_copy.wait), (27.0, send_moments)]
    for q, late in ((0, 0.0), (1, 5.0)):
        tasks += [
            (0.0, functools.partial(send_mirror, q)),
            (late + 3.8, functools.partial(recv_mirror, q)),
        ]
        tasks += gather(
            comm, ("basis", q),
            lambda xo, zo, q=q: bfull.at[q, yh, xo, zo],
            lambda xo, zo, q=q: bfull.at[q, 1 - yh, xo, zo],
            late, late + 3.9,
        )
        tasks += [
            (late + 16.5, functools.partial(project, q)),
            (late + 21.0, functools.partial(collect, q)),
            (late + 22.4, functools.partial(product, q)),
        ]
        tasks += scatters[q].steps(late + 24.0)
        tasks += [
            (late + 35.5, functools.partial(finish_half, q, 1)),
            (late + 36.5, functools.partial(finish_half, q, 0)),
            (late + 41.5, functools.partial(exchange, q)),
        ]
    run(tasks)
    g = gsum[...]

    sq = jnp.sum(g * g, axis=0, keepdims=True)
    part = sq[:, 0:128]
    for i in range(1, FFL // 128):
        part = part + sq[:, i * 128:(i + 1) * 128]
    n1[0] = part
    for j in range(NX):
        for k in range(NZ):
            if j or k:
                comm.send(
                    "n1", 0, n1.at[0], n1.at[j * NZ + k],
                    comm.dev(x=wrap(x + j, NX), z=wrap(z + k, NZ)),
                )
    comm.wait("n1", 0, n1.at[pl.ds(1, NX * NZ - 1)])
    n2[0] = jnp.sum(n1[...], axis=0)
    for r in range(NY):
        for e in range(2):
            if r or e:
                comm.send(
                    "n2", 0, n2.at[0], n2.at[r * 2 + e],
                    comm.dev(yl=wrap(yl + r, NY), c=lax.rem(c + e, 2)),
                )
    bas_copy.wait()
    row = lax.broadcasted_iota(jnp.int32, (R, R), 0)
    column = lax.broadcasted_iota(jnp.int32, (R, R), 1)
    source = ((column >> 3) & 1) * RH + (column >> 4) * BLK + (column & 7)
    pick = jnp.where(row == source, 1.0, 0.0).astype(jnp.bfloat16)
    bp[...] = jnp.dot(bas[...], pick, preferred_element_type=jnp.float32).astype(jnp.bfloat16)
    m_copy.wait()
    v_copy.wait()
    comm.wait("moments", 0)
    comm.wait("n2", 0, n2.at[pl.ds(1, NY * 2 - 1)])
    norm = jnp.sqrt(jnp.sum(jnp.sum(n2[...], axis=0), axis=1, keepdims=True))
    clipped = g * jnp.minimum(1.0, 1.0 / norm)
    new_first = 0.9 * mom[0] + 0.1 * clipped
    new_second = 0.999 * mom[1] + 0.001 * clipped * clipped
    first_fix = 1.0 - 0.9**20
    second_fix = 1.0 - 0.999**20
    direction = (new_first / first_fix / (jnp.sqrt(new_second / second_fix) + 1e-08)).astype(jnp.bfloat16)
    da[x, z] = direction[:, :WA]
    db[x, z] = direction[:, WA:]

    run(gather(comm, "direction", lambda xo, zo: da.at[xo, zo], lambda xo, zo: db.at[xo, zo], 0.0, 0.0))
    for start, full, width in ((0, da, WA), (WA, db, WB)):
        out_ref[:, pl.ds(start, width)] = jnp.dot(
            bp[...], full[...].reshape(R, width), preferred_element_type=jnp.float32
        )
    comm.sent("n1", n1.at[pl.ds(1, NX * NZ - 1)])
    comm.sent("n2", n2.at[pl.ds(1, NY * 2 - 1)])
    comm.finish()


N_PHASES, N_GROUPS = 18, 108


def local(tokens, up_cotangent, basis, first_moment, second_moment):
    bf, f32 = jnp.bfloat16, jnp.float32
    hbm_spec = pl.BlockSpec(memory_space=pltpu.HBM)
    vmem_spec = pl.BlockSpec(memory_space=pltpu.VMEM)
    return pl.pallas_call(
        kernel,
        out_shape=jax.ShapeDtypeStruct((BROWS, FFL), f32),
        in_specs=[hbm_spec] * 5,
        out_specs=vmem_spec,
        scratch_shapes=[
            pltpu.VMEM((2, TOK, 4096), bf),
            pltpu.VMEM((NY * 2 * TOK, FFL), bf),
            pltpu.VMEM((BROWS, R), bf),
            pltpu.VMEM((2, 2, NX, NZ, BROWS, RQ), bf),
            pltpu.VMEM((2, 2, NY, 2 * TOK, RQ), bf),
            pltpu.VMEM((2, RQ, NY * 2 * TOK), bf),
            pltpu.VMEM((2, RH, FFL), f32),
            pltpu.VMEM((2, 2 * BLK, FFL), f32),
            pltpu.VMEM((BROWS, R), bf),
            pltpu.VMEM((2, 2, 4, NX, 16, WA // 2), bf),
            pltpu.VMEM((2, 2, 4, NX, 16, WA // 2), bf),
            pltpu.VMEM((2, 2, 2, NZ, 16, WB // 2), bf),
            pltpu.VMEM((2, 2, 2, NZ, 16, WB // 2), bf),
            pltpu.VMEM((2, NX, 16, WA // 2), f32),
            pltpu.VMEM((2, NX, 16, WA // 2), bf),
            pltpu.VMEM((2, NX, 16, WA // 2), bf),
            pltpu.VMEM((2, NZ, 16, WB // 2), bf),
            pltpu.VMEM((2, NZ, 16, WB // 2), bf),
            pltpu.VMEM((2, 16, WA // 2), bf),
            pltpu.VMEM((2, 16, WA // 2), bf),
            pltpu.VMEM((2, 16, WB // 2), bf),
            pltpu.VMEM((2, 16, WB // 2), bf),
            pltpu.VMEM((2 * BLK, FFL), f32),
            pltpu.VMEM((NX * NZ, 1, 128), f32),
            pltpu.VMEM((NY * 2, 1, 128), f32),
            pltpu.VMEM((NX, NZ, 16, WA), bf),
            pltpu.VMEM((NX, NZ, 16, WB), bf),
            pltpu.VMEM((UNITS, 16, 128), bf),
            pltpu.SemaphoreType.DMA((7,)),
            pltpu.SemaphoreType.DMA((N_PHASES,)),
            pltpu.SemaphoreType.DMA((N_GROUPS,)),
        ],
        compiler_params=pltpu.CompilerParams(
            collective_id=0, has_side_effects=True, vmem_limit_bytes=63 * 2**20
        ),
        cost_estimate=pl.CostEstimate(flops=4 * 10**9, bytes_accessed=2 * 10**7, transcendentals=0),
        name="galore_step",
    )(tokens, up_cotangent, basis, first_moment, second_moment)


def solution(mesh):
    in_specs = (
        P(("dp", "tensor"), None),
        P("dp", "tensor"),
        P("dp", None),
        P("dp", "tensor"),
        P("dp", "tensor"),
    )
    out_specs = P("dp", "tensor")
    return jax.shard_map(local, mesh=mesh, in_specs=in_specs, out_specs=out_specs, check_vma=False)
```

```python
import functools

import jax
import jax.numpy as jnp
from jax import lax
from jax.experimental import pallas as pl
from jax.experimental.pallas import tpu as pltpu
from jax.sharding import PartitionSpec as P

MESH = pl.DeviceIdType.MESH
NX, NZ, NY = 4, 8, 4
BLK = 8
TOK = 96
FFL = 1792
WA, WB = 768, 1024
R = 512
RH = R // 2
RQ = RH // 2
BROWS = 64
X_ORDER = (0, 1, 3, 2)
Z_ORDER = (0, 1, -1, 2, -2, 3, -3, 4)
ZH = {1: (0, 1, 2, 3), -1: (-1, -2, -3, 4)}
XH = {1: (0, 1), -1: (3, 2)}
RZH = {1: (3, 1, 2, 0), -1: (4, -3, -1, -2)}
RXH = {1: (0, 2), -1: (1, 3)}
SIDES = (1, -1)


UNIT = 16 * 128 * 2
UNITS = 320


class Comm:
    def __init__(self, ssem, rsem, tally, coords):
        self.ssem, self.rsem, self.tally, self.coords = ssem, rsem, tally, coords
        self.groups, self.phases, self.coming, self.going = {}, {}, {}, {}

    def dev(self, yh=None, x=None, z=None, yl=None, c=None):
        own = self.coords
        yh, x, z, yl, c = (o if v is None else v for v, o in zip((yh, x, z, yl, c), own))
        return (yh * 32 + x * 8 + z, yl * 2 + c)

    def send(self, phase, group, src, dst, dev):
        i = self.phases.setdefault(phase, len(self.phases))
        j = self.groups.setdefault((phase, group), len(self.groups))
        pltpu.make_async_remote_copy(
            src_ref=src, dst_ref=dst, send_sem=self.ssem.at[i], recv_sem=self.rsem.at[j],
            device_id=dev, device_id_type=MESH,
        ).start()
        size = src.dtype.itemsize
        for n in src.shape:
            size *= n
        self.going[phase] = self.going.get(phase, 0) + size
        self.coming[phase, group] = self.coming.get((phase, group), 0) + size

    def total(self, size, ref):
        if ref is None:
            assert size % UNIT == 0 and size <= UNIT * UNITS
            ref = self.tally.at[pl.ds(0, size // UNIT)]
        return ref

    def wait(self, phase, group, ref=None):
        ref = self.total(self.coming.pop((phase, group)), ref)
        j = self.groups[phase, group]
        pltpu.make_async_remote_copy(
            src_ref=ref, dst_ref=ref, send_sem=self.ssem.at[0], recv_sem=self.rsem.at[j],
            device_id=self.dev(), device_id_type=MESH,
        ).wait_recv()

    def sent(self, phase, ref=None):
        ref = self.total(self.going.pop(phase), ref)
        pltpu.make_async_remote_copy(
            src_ref=ref, dst_ref=ref, send_sem=self.ssem.at[self.phases[phase]], recv_sem=self.rsem.at[0],
            device_id=self.dev(), device_id_type=MESH,
        ).wait_send()

    def finish(self):
        for phase in list(self.going):
            self.sent(phase)


def wrap(v, n):
    return lax.rem(v + n, n)


def run(tasks):
    for _, step in sorted(tasks, key=lambda task: task[0]):
        step()


def gather(comm, name, view_a, view_b, begin, begin_b):
    _, x, z, _, c = comm.coords
    turn = 1 - 2 * c

    def zs(k):
        return wrap(z + turn * k, NZ)

    near = {0: 0, 1: 1, 3: 1, 2: 2}
    far = {0: 0, 1: 1, -1: 1, 2: 2, -2: 2, 3: 3, -3: 3, 4: 3}
    name_a, name_b = (name, "a"), (name, "b")

    def send_ax():
        for j in X_ORDER[1:]:
            comm.send(name_a, ("x", near[j]), view_a(x, z), view_a(x, z), comm.dev(x=wrap(x + j, NX)))

    def ring_a(s, js):
        if s == 1 and js[0]:
            comm.wait(name_a, ("x", near[js[0]]))
        if 1 < s < 5:
            comm.wait(name_a, ("z", s - 1, near[js[0]]))
        if s == 5:
            comm.wait(name_a, ("z", 4))
            return
        for j in js:
            xo = wrap(x - j, NX)
            for side in SIDES:
                zo = wrap(z - side * (s - 1), NZ)
                if s < 4 or j in XH[side]:
                    group = ("z", s, near[j]) if s < 4 else ("z", 4)
                    comm.send(name_a, group, view_a(xo, zo), view_a(xo, zo), comm.dev(z=wrap(z + side, NZ)))

    def send_b(k, origin, hop):
        comm.send(name_b, ("z", far[k]), view_b(x, origin), view_b(x, origin), comm.dev(z=zs(hop)))

    def send_bz():
        for k in (2, -2, 1, -1):
            send_b(k, z, k)

    def ring_b1(ks):
        if ks[0]:
            comm.wait(name_b, ("z", far[ks[0]]))
        for k in ks:
            zo = zs(-k)
            if k == 2:
                send_b(3, zo, 1)
                send_b(4, zo, 2)
            if k == -2:
                send_b(-3, zo, -1)
            for side in SIDES:
                comm.send(name_b, ("x", far[k]), view_b(x, zo), view_b(x, zo), comm.dev(x=wrap(x + side, NX)))

    def ring_b2(ks):
        comm.wait(name_b, ("x", far[ks[0]]))
        for k in ks:
            zo = zs(-k)
            for side in SIDES:
                xo = wrap(x - side, NX)
                if k in ZH[side]:
                    comm.send(name_b, "x2", view_b(xo, zo), view_b(xo, zo), comm.dev(x=wrap(x + side, NX)))

    def last_b():
        comm.wait(name_b, "x2")

    steps_a = [
        (0.0, send_ax), (0.0, lambda: ring_a(1, (0,))),
        (2.3, lambda: ring_a(2, (0,))), (2.4, lambda: ring_a(1, (1, 3))), (2.9, lambda: ring_a(1, (2,))),
        (4.6, lambda: ring_a(3, (0,))), (4.7, lambda: ring_a(2, (1, 3))), (5.2, lambda: ring_a(2, (2,))),
        (7.0, lambda: ring_a(4, (0,))), (7.2, lambda: ring_a(3, (1, 3))), (7.6, lambda: ring_a(3, (2,))),
        (9.5, lambda: ring_a(4, (1, 3))), (9.9, lambda: ring_a(4, (2,))), (12.3, lambda: ring_a(5, X_ORDER)),
    ]
    steps_b = [
        (0.0, send_bz), (0.0, lambda: ring_b1((0,))),
        (2.3, lambda: ring_b1((1, -1))), (2.4, lambda: ring_b2((0,))), (3.0, lambda: ring_b1((2, -2))),
        (4.7, lambda: ring_b2((1, -1))), (5.4, lambda: ring_b2((2, -2))), (6.0, lambda: ring_b1((3, -3, 4))),
        (8.5, lambda: ring_b2((3, -3, 4))), (10.7, last_b),
    ]
    return [(begin + 1.4 * t, f) for t, f in steps_a] + [(begin_b + 1.4 * t, f) for t, f in steps_b]


class Scatter:
    def __init__(self, comm, name, block, sa, ra, sb, rb, asum, sax, rax, sbz, rbz):
        self.comm, self.name_a, self.name_b, self.block = comm, (name, "a"), (name, "b"), block
        self.last = {0: 0, 1: 1, -1: 1, 2: 2, -2: 2, 3: 3, -3: 3, 4: 3}
        self.sa, self.ra, self.sb, self.rb = sa, ra, sb, rb
        self.asum, self.sax, self.rax, self.sbz, self.rbz = asum, sax, rax, sbz, rbz
        _, self.x, self.z, _, c = comm.coords
        self.turn = 1 - 2 * c

    def zs(self, k):
        return wrap(self.z + self.turn * k, NZ)

    def step_a(self, s, prior):
        comm = self.comm
        if s >= 2 or prior and s:
            comm.wait(self.name_a, (s - 1, prior))
        for n, side in enumerate(SIDES):
            for j in RXH[side if prior else -side]:
                value = self.block(0, j, wrap(self.z + side * (4 - s), NZ))
                if s >= 2 or prior and s:
                    value = value + self.ra[n, s - 1, j].astype(jnp.float32)
                out = self.sa.at[n, s, j]
                out[...] = value.astype(jnp.bfloat16)
                group = (s, prior) if s < 3 else 3
                comm.send(self.name_a, group, out, self.ra.at[n, s, j], comm.dev(z=wrap(self.z + side, NZ)))

    def step_b(self, s, prior, part):
        comm = self.comm
        if s and prior:
            comm.wait(self.name_b, (0, part))
        for n, side in enumerate(SIDES):
            for k in RZH[side if prior else -side][2 * part:2 * part + 2]:
                value = self.block(1, wrap(self.x + side * (2 - s), NX), self.zs(k))
                if s and prior:
                    value = value + self.rb[n, 0, k % NZ].astype(jnp.float32)
                out = self.sb.at[n, s, k % NZ]
                out[...] = value.astype(jnp.bfloat16)
                group = (1, self.last[k]) if s else (0, part)
                comm.send(self.name_b, group, out, self.rb.at[n, s, k % NZ], comm.dev(x=wrap(self.x + side, NX)))

    def last_a(self):
        comm = self.comm
        comm.wait(self.name_a, 3)
        for j in range(NX):
            value = self.block(0, j, self.z)
            for n in range(2):
                value = value + self.ra[n, 3, j].astype(jnp.float32)
            self.asum[j] = value
            self.sax[j] = value.astype(jnp.bfloat16)
        for j in (2, 1, 3):
            xo = wrap(self.x + j, NX)
            comm.send(self.name_a, "x", self.sax.at[xo], self.rax.at[j], comm.dev(x=xo))

    def total_a(self):
        value = self.asum[self.x]
        self.comm.wait(self.name_a, "x")
        for j in (1, 3, 2):
            value = value + self.rax[j].astype(jnp.float32)
        return value

    def last_b(self, ks):
        comm = self.comm
        hop = {3: 1, -3: -1, 4: 2}
        plus = {2: (3, 4), -2: (-3,), 0: (1, -1, 2, -2)}
        comm.wait(self.name_b, (1, self.last[ks[0]]))
        if ks[0] in (0, 2):
            comm.wait(self.name_b, ("z", ks[0]))
        for k in ks:
            value = self.block(1, self.x, self.zs(k))
            for n in range(2):
                value = value + self.rb[n, 1, k % NZ].astype(jnp.float32)
            for other in plus.get(k, ()):
                value = value + self.rbz[other % NZ].astype(jnp.float32)
            if k == 0:
                return value
            self.sbz[k % NZ] = value.astype(jnp.bfloat16)
            comm.send(
                self.name_b, ("z", 2 if k in hop else 0), self.sbz.at[k % NZ], self.rbz.at[k % NZ],
                comm.dev(z=self.zs(hop.get(k, k))),
            )

    def steps(self, begin):
        a, b = self.step_a, self.step_b
        steps = [
            (0.0, lambda: a(0, True)), (0.0, lambda: b(0, True, 0)), (0.1, lambda: b(0, True, 1)),
            (0.2, lambda: a(1, False)), (0.3, lambda: b(1, False, 0)), (0.3, lambda: b(1, False, 1)),
            (2.3, lambda: a(1, True)), (2.5, lambda: a(2, False)),
            (2.6, lambda: b(1, True, 0)), (2.9, lambda: b(1, True, 1)),
            (4.6, lambda: a(2, True)), (4.9, lambda: a(3, False)),
            (5.2, lambda: self.last_b((4, 3, -3))), (5.8, lambda: self.last_b((1, -1))),
            (7.0, lambda: a(3, True)), (8.5, lambda: self.last_b((2, -2))), (9.4, self.last_a),
        ]
        return [(begin + 1.3 * t, f) for t, f in steps]


def kernel(
    tok_ref, up_ref, basis_ref, m_ref, v_ref, out_ref,
    toks, upv, bas, bfull, pall, pt, grad, mom, bp,
    sa, ra, sb, rb, asum, sax, rax, sbz, rbz, ysa, yra, ysb, yrb, gsum, n1, n2, da, db,
    tally, lsem, ssem, rsem,
):
    d, t = lax.axis_index("dp"), lax.axis_index("tensor")
    yh, x, z, yl, c = lax.div(d, 32), lax.rem(lax.div(d, 8), 4), lax.rem(d, 8), lax.div(t, 2), lax.rem(t, 2)
    comm = Comm(ssem, rsem, tally, (yh, x, z, yl, c))
    other_core = comm.dev(c=1 - c)
    other_run = comm.dev(yh=1 - yh)
    mirror = comm.dev(yh=1 - yh, yl=3 - yl)

    b_copies = []
    for q in range(2):
        columns = pl.ds(pl.multiple_of(q * RH + c * RQ, RQ), RQ)
        b_copies.append(pltpu.make_async_copy(basis_ref.at[:, columns], bfull.at[q, yh, x, z], lsem.at[5 + q]))
        b_copies[q].start()
    barrier = pltpu.get_barrier_semaphore()
    peers = [other_core, mirror]
    peers += [comm.dev(x=wrap(x + j, NX)) for j in range(1, NX)]
    peers += [comm.dev(z=wrap(z + k, NZ)) for k in (1, -1, 2, -2)]
    peers += [comm.dev(yl=wrap(yl + r, NY)) for r in range(1, NY)]
    for peer in peers:
        pl.semaphore_signal(barrier, inc=1, device_id=peer, device_id_type=MESH)

    row0 = pl.multiple_of(yh * BLK, BLK)
    tok_copy = pltpu.make_async_copy(tok_ref, toks.at[c], lsem.at[0])
    up_copy = pltpu.make_async_copy(up_ref, upv, lsem.at[1])
    m_copy = pltpu.make_async_copy(m_ref, mom.at[0, pl.ds(row0, BLK)], lsem.at[2])
    v_copy = pltpu.make_async_copy(v_ref, mom.at[1, pl.ds(row0, BLK)], lsem.at[3])
    bas_copy = pltpu.make_async_copy(basis_ref, bas, lsem.at[4])
    for copy in b_copies:
        copy.wait()
    pl.semaphore_wait(barrier, len(peers))

    def send_mirror(q):
        comm.send("mirror", q, bfull.at[q, yh, x, z], bfull.at[q, yh, x, z], mirror)

    def recv_mirror(q):
        comm.wait("mirror", q)

    def load_rest():
        for copy in (up_copy, m_copy, v_copy, bas_copy):
            copy.start()

    def send_tokens():
        tok_copy.start()
        comm.send("tok", 0, tok_ref, toks.at[c], other_core)

    def recv_tokens():
        tok_copy.wait()
        comm.wait("tok", 0)

    def send_moments():
        comm.send("moments", 0, m_ref, mom.at[0, pl.ds(row0, BLK)], other_run)
        comm.send("moments", 0, v_ref, mom.at[1, pl.ds(row0, BLK)], other_run)

    def project(q):
        proj = jnp.zeros((2 * TOK, RQ), jnp.float32)
        depth = NZ * BROWS
        for a in range(2):
            for b in range(NX):
                left = toks[:, :, pl.ds((a * NX + b) * depth, depth)].reshape(2 * TOK, depth)
                proj += jnp.dot(left, bfull[q, a, b].reshape(depth, RQ), preferred_element_type=jnp.float32)
        piece = pall.at[q, c, yl]
        piece[...] = proj.astype(jnp.bfloat16)
        for r in (2, 1, 3):
            comm.send("p", (q, r % 2), piece, piece, comm.dev(yl=wrap(yl + r, NY)))
        comm.send("core", q, piece, piece, other_core)

    def collect(q):
        for r in (1, 3, 2):
            piece = pall.at[q, c, wrap(yl - r, NY)]
            if r != 3:
                comm.wait("p", (q, r % 2))
            comm.send("core", q, piece, piece, other_core)

    def product(q):
        comm.wait("core", q)
        for half in range(2):
            pt[half] = pall[q, half].reshape(NY * 2 * TOK, RQ).T

        def tile(i, carry):
            columns = pl.ds(pl.multiple_of(i * 256, 256), 256)
            left = pt[...].reshape(RH, NY * 2 * TOK)
            grad[q, :, columns] = jnp.dot(left, upv[:, columns], preferred_element_type=jnp.float32)
            return carry

        lax.fori_loop(0, FFL // 256, tile, 0)

    def block_of(q):
        def block(half, xo, zo):
            rows = pl.ds(pl.multiple_of((xo * NZ + zo) * BLK, BLK), BLK)
            start, width = (WA, WB // 2) if half else (0, WA // 2)
            parts = [grad[q, rows, pl.ds(start + i * width, width)] for i in range(2)]
            return jnp.concatenate(parts, axis=0)

        return block

    scatters = [
        Scatter(
            comm, ("rs", q), block_of(q),
            *(ref.at[q] for ref in (sa, ra, sb, rb, asum, sax, rax, sbz, rbz)),
        )
        for q in range(2)
    ]
    sums = [[None, None], [None, None]]

    def finish_half(q, half):
        value = scatters[q].last_b((0,)) if half else scatters[q].total_a()
        ys, yr = ((ysa, yra), (ysb, yrb))[half]
        ys[q] = value.astype(jnp.bfloat16)
        comm.send("y", (q, half), ys.at[q], yr.at[q], other_run)
        sums[q][half] = value

    def exchange(q):
        rows = pl.ds(q * BLK, BLK)
        for half, (yr, start, width) in enumerate(((yra, 0, WA // 2), (yrb, WA, WB // 2))):
            comm.wait("y", (q, half))
            value = (sums[q][half] + yr[q].astype(jnp.float32)) * (1.0 / (NY * 2 * TOK * 64))
            for i in range(2):
                gsum[rows, pl.ds(start + i * width, width)] = value[i * BLK:(i + 1) * BLK]

    tasks = [(2.0, send_tokens), (7.0, load_rest), (19.6, recv_tokens), (27.2, up_copy.wait), (37.0, send_moments)]
    for q, late in ((0, 0.0), (1, 7.5)):
        tasks += [
            (0.6 * late, functools.partial(send_mirror, q)),
            (late + 4.4, functools.partial(recv_mirror, q)),
        ]
        tasks += gather(
            comm, ("basis", q),
            lambda xo, zo, q=q: bfull.at[q, yh, xo, zo],
            lambda xo, zo, q=q: bfull.at[q, 1 - yh, xo, zo],
            late, late + 4.5,
        )
        tasks += [
            (late + 19.7, functools.partial(project, q)),
            (late + 25.7, functools.partial(collect, q)),
            (late + 27.3, functools.partial(product, q)),
        ]
        tasks += scatters[q].steps(late + 28.8)
        tasks += [
            (late + 43.8, functools.partial(finish_half, q, 1)),
            (late + 45.0, functools.partial(finish_half, q, 0)),
            (late + 50.0, functools.partial(exchange, q)),
        ]
    run(tasks)
    g = gsum[...]

    sq = jnp.sum(g * g, axis=0, keepdims=True)
    part = sq[:, 0:128]
    for i in range(1, FFL // 128):
        part = part + sq[:, i * 128:(i + 1) * 128]
    n1[0] = part
    for j in range(NX):
        for k in range(NZ):
            if j or k:
                comm.send(
                    "n1", 0, n1.at[0], n1.at[j * NZ + k],
                    comm.dev(x=wrap(x + j, NX), z=wrap(z + k, NZ)),
                )
    comm.wait("n1", 0, n1.at[pl.ds(1, NX * NZ - 1)])
    n2[0] = jnp.sum(n1[...], axis=0)
    for r in range(NY):
        for e in range(2):
            if r or e:
                comm.send(
                    "n2", 0, n2.at[0], n2.at[r * 2 + e],
                    comm.dev(yl=wrap(yl + r, NY), c=lax.rem(c + e, 2)),
                )
    bas_copy.wait()
    row = lax.broadcasted_iota(jnp.int32, (R, R), 0)
    column = lax.broadcasted_iota(jnp.int32, (R, R), 1)
    source = ((column >> 3) & 1) * RH + (column >> 4) * BLK + (column & 7)
    pick = jnp.where(row == source, 1.0, 0.0).astype(jnp.bfloat16)
    bp[...] = jnp.dot(bas[...], pick, preferred_element_type=jnp.float32).astype(jnp.bfloat16)
    m_copy.wait()
    v_copy.wait()
    comm.wait("moments", 0)
    comm.wait("n2", 0, n2.at[pl.ds(1, NY * 2 - 1)])
    norm = jnp.sqrt(jnp.sum(jnp.sum(n2[...], axis=0), axis=1, keepdims=True))
    clipped = g * jnp.minimum(1.0, 1.0 / norm)
    new_first = 0.9 * mom[0] + 0.1 * clipped
    new_second = 0.999 * mom[1] + 0.001 * clipped * clipped
    first_fix = 1.0 - 0.9**20
    second_fix = 1.0 - 0.999**20
    direction = (new_first / first_fix / (jnp.sqrt(new_second / second_fix) + 1e-08)).astype(jnp.bfloat16)
    da[x, z] = direction[:, :WA]
    db[x, z] = direction[:, WA:]

    run(gather(comm, "direction", lambda xo, zo: da.at[xo, zo], lambda xo, zo: db.at[xo, zo], 0.0, 0.0))
    for start, full, width in ((0, da, WA), (WA, db, WB)):
        out_ref[:, pl.ds(start, width)] = jnp.dot(
            bp[...], full[...].reshape(R, width), preferred_element_type=jnp.float32
        )
    comm.sent("n1", n1.at[pl.ds(1, NX * NZ - 1)])
    comm.sent("n2", n2.at[pl.ds(1, NY * 2 - 1)])
    comm.finish()


N_PHASES, N_GROUPS = 18, 108


def local(tokens, up_cotangent, basis, first_moment, second_moment):
    bf, f32 = jnp.bfloat16, jnp.float32
    hbm_spec = pl.BlockSpec(memory_space=pltpu.HBM)
    vmem_spec = pl.BlockSpec(memory_space=pltpu.VMEM)
    return pl.pallas_call(
        kernel,
        out_shape=jax.ShapeDtypeStruct((BROWS, FFL), f32),
        in_specs=[hbm_spec] * 5,
        out_specs=vmem_spec,
        scratch_shapes=[
            pltpu.VMEM((2, TOK, 4096), bf),
            pltpu.VMEM((NY * 2 * TOK, FFL), bf),
            pltpu.VMEM((BROWS, R), bf),
            pltpu.VMEM((2, 2, NX, NZ, BROWS, RQ), bf),
            pltpu.VMEM((2, 2, NY, 2 * TOK, RQ), bf),
            pltpu.VMEM((2, RQ, NY * 2 * TOK), bf),
            pltpu.VMEM((2, RH, FFL), f32),
            pltpu.VMEM((2, 2 * BLK, FFL), f32),
            pltpu.VMEM((BROWS, R), bf),
            pltpu.VMEM((2, 2, 4, NX, 16, WA // 2), bf),
            pltpu.VMEM((2, 2, 4, NX, 16, WA // 2), bf),
            pltpu.VMEM((2, 2, 2, NZ, 16, WB // 2), bf),
            pltpu.VMEM((2, 2, 2, NZ, 16, WB // 2), bf),
            pltpu.VMEM((2, NX, 16, WA // 2), f32),
            pltpu.VMEM((2, NX, 16, WA // 2), bf),
            pltpu.VMEM((2, NX, 16, WA // 2), bf),
            pltpu.VMEM((2, NZ, 16, WB // 2), bf),
            pltpu.VMEM((2, NZ, 16, WB // 2), bf),
            pltpu.VMEM((2, 16, WA // 2), bf),
            pltpu.VMEM((2, 16, WA // 2), bf),
            pltpu.VMEM((2, 16, WB // 2), bf),
            pltpu.VMEM((2, 16, WB // 2), bf),
            pltpu.VMEM((2 * BLK, FFL), f32),
            pltpu.VMEM((NX * NZ, 1, 128), f32),
            pltpu.VMEM((NY * 2, 1, 128), f32),
            pltpu.VMEM((NX, NZ, 16, WA), bf),
            pltpu.VMEM((NX, NZ, 16, WB), bf),
            pltpu.VMEM((UNITS, 16, 128), bf),
            pltpu.SemaphoreType.DMA((7,)),
            pltpu.SemaphoreType.DMA((N_PHASES,)),
            pltpu.SemaphoreType.DMA((N_GROUPS,)),
        ],
        compiler_params=pltpu.CompilerParams(
            collective_id=0, has_side_effects=True, vmem_limit_bytes=63 * 2**20
        ),
        cost_estimate=pl.CostEstimate(flops=4 * 10**9, bytes_accessed=2 * 10**7, transcendentals=0),
        name="galore_step",
    )(tokens, up_cotangent, basis, first_moment, second_moment)


def solution(mesh):
    in_specs = (
        P(("dp", "tensor"), None),
        P("dp", "tensor"),
        P("dp", None),
        P("dp", "tensor"),
        P("dp", "tensor"),
    )
    out_specs = P("dp", "tensor")
    return jax.shard_map(local, mesh=mesh, in_specs=in_specs, out_specs=out_specs, check_vma=False)
```

```python
import functools

import jax
import jax.numpy as jnp
from jax import lax
from jax.experimental import pallas as pl
from jax.experimental.pallas import tpu as pltpu
from jax.sharding import PartitionSpec as P

MESH = pl.DeviceIdType.MESH
NX, NZ, NY = 4, 8, 4
BLK = 8
TOK = 96
FFL = 1792
WA, WB = 512, 1280
DA, DB = 640, 1152
R = 512
RH = R // 2
RQ = RH // 2
BROWS = 64
X_ORDER = (0, 1, 3, 2)
Z_ORDER = (0, 1, -1, 2, -2, 3, -3, 4)
RZH = {1: (3, 1, 2, 0), -1: (4, -3, -1, -2)}
SIDES = (1, -1)


UNIT = 16 * 128 * 2
UNITS = 320


class Comm:
    def __init__(self, ssem, rsem, tally, coords):
        self.ssem, self.rsem, self.tally, self.coords = ssem, rsem, tally, coords
        self.groups, self.phases, self.coming, self.going = {}, {}, {}, {}

    def dev(self, yh=None, x=None, z=None, yl=None, c=None):
        own = self.coords
        yh, x, z, yl, c = (o if v is None else v for v, o in zip((yh, x, z, yl, c), own))
        return (yh * 32 + x * 8 + z, yl * 2 + c)

    def send(self, phase, group, src, dst, dev):
        i = self.phases.setdefault(phase, len(self.phases))
        j = self.groups.setdefault((phase, group), len(self.groups))
        pltpu.make_async_remote_copy(
            src_ref=src, dst_ref=dst, send_sem=self.ssem.at[i], recv_sem=self.rsem.at[j],
            device_id=dev, device_id_type=MESH,
        ).start()
        size = src.dtype.itemsize
        for n in src.shape:
            size *= n
        self.going[phase] = self.going.get(phase, 0) + size
        self.coming[phase, group] = self.coming.get((phase, group), 0) + size

    def total(self, size, ref):
        if ref is None:
            assert size % UNIT == 0 and size <= UNIT * UNITS
            ref = self.tally.at[pl.ds(0, size // UNIT)]
        return ref

    def wait(self, phase, group, ref=None):
        ref = self.total(self.coming.pop((phase, group)), ref)
        j = self.groups[phase, group]
        pltpu.make_async_remote_copy(
            src_ref=ref, dst_ref=ref, send_sem=self.ssem.at[0], recv_sem=self.rsem.at[j],
            device_id=self.dev(), device_id_type=MESH,
        ).wait_recv()

    def sent(self, phase, ref=None):
        ref = self.total(self.going.pop(phase), ref)
        pltpu.make_async_remote_copy(
            src_ref=ref, dst_ref=ref, send_sem=self.ssem.at[self.phases[phase]], recv_sem=self.rsem.at[0],
            device_id=self.dev(), device_id_type=MESH,
        ).wait_send()

    def finish(self):
        for phase in list(self.going):
            self.sent(phase)


def wrap(v, n):
    return lax.rem(v + n, n)


def run(tasks):
    for _, step in sorted(tasks, key=lambda task: task[0]):
        step()


def gather(comm, name, view_a, view_b, begin, begin_b):
    _, x, z, _, c = comm.coords
    turn = 1 - 2 * c

    def zs(k):
        return wrap(z + turn * k, NZ)

    near = {0: 0, 1: 1, 3: 1, 2: 2}
    far = {0: 0, 1: 1, -1: 1, 2: 2, -2: 2, 3: 3, -3: 3, 4: 3}
    name_a, name_b = (name, "a"), (name, "b")

    def send_ax():
        for j in X_ORDER[1:]:
            comm.send(name_a, ("x", near[j]), view_a(x, z), view_a(x, z), comm.dev(x=wrap(x + j, NX)))

    def pass_a(xo, origin, hop, group):
        comm.send(name_a, group, view_a(xo, origin), view_a(xo, origin), comm.dev(z=zs(hop)))

    def near_a(js):
        if js[0]:
            comm.wait(name_a, ("x", near[js[0]]))
        for j in js:
            xo = wrap(x - j, NX)
            for hop in (2, -2, 1, -1):
                pass_a(xo, z, hop, ("z", near[j]) if hop in (2, -2) else "z")

    def far_a(js):
        comm.wait(name_a, ("z", near[js[0]]))
        for j in js:
            xo = wrap(x - j, NX)
            pass_a(xo, zs(-2), 2, "z")
            pass_a(xo, zs(-2), 1, "z")
            pass_a(xo, zs(2), -1, "z")

    def last_a():
        comm.wait(name_a, "z")

    def send_b(k, origin, hop):
        comm.send(name_b, ("z", far[k]), view_b(x, origin), view_b(x, origin), comm.dev(z=zs(hop)))

    def send_bz():
        for k in (2, -2, 1, -1):
            send_b(k, z, k)

    def cross_b(ks):
        if ks[0]:
            comm.wait(name_b, ("z", far[ks[0]]))
        for k in ks:
            zo = zs(-k)
            if k == 2:
                send_b(4, zo, 2)
                send_b(3, zo, 1)
            if k == -2:
                send_b(-3, zo, -1)
        for k in ks:
            zo = zs(-k)
            for j in X_ORDER[1:]:
                comm.send(name_b, "x", view_b(x, zo), view_b(x, zo), comm.dev(x=wrap(x + j, NX)))

    def last_b():
        comm.wait(name_b, "x")

    steps_a = [
        (0.0, send_ax), (0.0, lambda: near_a((0,))), (2.8, lambda: near_a((1, 3))), (3.3, lambda: far_a((0,))),
        (3.4, lambda: near_a((2,))), (6.2, lambda: far_a((1, 3))), (6.9, lambda: far_a((2,))), (11.0, last_a),
    ]
    steps_b = [
        (0.0, send_bz), (0.0, lambda: cross_b((0,))), (3.3, lambda: cross_b((2, -2))), (3.4, lambda: cross_b((1, -1))),
        (6.8, lambda: cross_b((4, 3, -3))), (11.0, last_b),
    ]
    return [(begin + t, f) for t, f in steps_a] + [(begin_b + t, f) for t, f in steps_b]


class Scatter:
    def __init__(self, comm, name, block, sa, ra, sb, rb, asum, sax, rax, sbz, rbz):
        self.comm, self.name_a, self.name_b, self.block = comm, (name, "a"), (name, "b"), block
        self.last = {0: 0, 1: 1, -1: 1, 2: 2, -2: 2, 3: 3, -3: 3, 4: 3}
        self.sa, self.ra, self.sb, self.rb = sa, ra, sb, rb
        self.asum, self.sax, self.rax, self.sbz, self.rbz = asum, sax, rax, sbz, rbz
        _, self.x, self.z, _, c = comm.coords
        self.turn = 1 - 2 * c

    def zs(self, k):
        return wrap(self.z + self.turn * k, NZ)

    def pass_a(self, j, k, hop, others, group):
        value = self.block(0, j, self.zs(k))
        for other in others:
            value = value + self.ra[other % NZ, j].astype(jnp.float32)
        out = self.sa.at[k % NZ, j]
        out[...] = value.astype(jnp.bfloat16)
        self.comm.send(self.name_a, group, out, self.ra.at[k % NZ, j], self.comm.dev(z=self.zs(hop)))

    def far_a(self, part):
        for j in (2 * part, 2 * part + 1):
            self.pass_a(j, 4, 2, (), ("far", part))
            self.pass_a(j, 3, 1, (), ("far", part))
            self.pass_a(j, -3, -1, (), ("far", part))

    def near_a(self, part):
        for j in (2 * part, 2 * part + 1):
            self.pass_a(j, 1, 1, (), "near")
            self.pass_a(j, -1, -1, (), "near")

    def mid_a(self, part):
        self.comm.wait(self.name_a, ("far", part))
        for j in (2 * part, 2 * part + 1):
            self.pass_a(j, 2, 2, (3, 4), "near")
            self.pass_a(j, -2, -2, (-3,), "near")

    def step_b(self, s, prior, part):
        comm = self.comm
        if s and prior:
            comm.wait(self.name_b, (0, part))
        for n, side in enumerate(SIDES):
            for k in RZH[side if prior else -side][2 * part:2 * part + 2]:
                value = self.block(1, wrap(self.x + side * (2 - s), NX), self.zs(k))
                if s and prior:
                    value = value + self.rb[n, 0, k % NZ].astype(jnp.float32)
                out = self.sb.at[n, s, k % NZ]
                out[...] = value.astype(jnp.bfloat16)
                group = (1, self.last[k]) if s else (0, part)
                comm.send(self.name_b, group, out, self.rb.at[n, s, k % NZ], comm.dev(x=wrap(self.x + side, NX)))

    def last_a(self):
        comm = self.comm
        comm.wait(self.name_a, "near")
        for j in range(NX):
            value = self.block(0, j, self.z)
            for k in (1, -1, 2, -2):
                value = value + self.ra[k % NZ, j].astype(jnp.float32)
            self.asum[j] = value
            self.sax[j] = value.astype(jnp.bfloat16)
        for j in (2, 1, 3):
            xo = wrap(self.x + j, NX)
            comm.send(self.name_a, "x", self.sax.at[xo], self.rax.at[j], comm.dev(x=xo))

    def total_a(self):
        value = self.asum[self.x]
        self.comm.wait(self.name_a, "x")
        for j in (1, 3, 2):
            value = value + self.rax[j].astype(jnp.float32)
        return value

    def last_b(self, ks):
        comm = self.comm
        hop = {3: 1, -3: -1, 4: 2}
        plus = {2: (3, 4), -2: (-3,), 0: (1, -1, 2, -2)}
        comm.wait(self.name_b, (1, self.last[ks[0]]))
        if ks[0] in (0, 2):
            comm.wait(self.name_b, ("z", ks[0]))
        for k in ks:
            value = self.block(1, self.x, self.zs(k))
            for n in range(2):
                value = value + self.rb[n, 1, k % NZ].astype(jnp.float32)
            for other in plus.get(k, ()):
                value = value + self.rbz[other % NZ].astype(jnp.float32)
            if k == 0:
                return value
            self.sbz[k % NZ] = value.astype(jnp.bfloat16)
            comm.send(
                self.name_b, ("z", 2 if k in hop else 0), self.sbz.at[k % NZ], self.rbz.at[k % NZ],
                comm.dev(z=self.zs(hop.get(k, k))),
            )

    def steps(self, begin):
        b = self.step_b
        steps = [
            (0.0, lambda: self.far_a(0)), (0.1, lambda: b(0, True, 0)), (0.2, lambda: self.far_a(1)),
            (0.3, lambda: b(0, True, 1)), (0.4, lambda: self.near_a(0)), (0.5, lambda: b(1, False, 0)),
            (0.6, lambda: self.near_a(1)), (0.7, lambda: b(1, False, 1)),
            (3.4, lambda: self.mid_a(0)), (3.5, lambda: b(1, True, 0)),
            (3.6, lambda: self.mid_a(1)), (3.8, lambda: b(1, True, 1)),
            (6.9, self.last_a), (7.0, lambda: self.last_b((4, 3, -3))), (7.5, lambda: self.last_b((1, -1))),
            (10.4, lambda: self.last_b((2, -2))),
        ]
        return [(begin + t, f) for t, f in steps]


def kernel(
    tok_ref, up_ref, basis_ref, m_ref, v_ref, out_ref,
    toks, upv, bas, bfull, pall, pt, grad, mom, bp,
    sa, ra, sb, rb, asum, sax, rax, sbz, rbz, ysa, yra, ysb, yrb, gsum, n1, n2, da, db,
    tally, lsem, ssem, rsem,
):
    d, t = lax.axis_index("dp"), lax.axis_index("tensor")
    yh, x, z, yl, c = lax.div(d, 32), lax.rem(lax.div(d, 8), 4), lax.rem(d, 8), lax.div(t, 2), lax.rem(t, 2)
    comm = Comm(ssem, rsem, tally, (yh, x, z, yl, c))
    other_core = comm.dev(c=1 - c)
    other_run = comm.dev(yh=1 - yh)
    mirror = comm.dev(yh=1 - yh, yl=3 - yl)

    b_copies = []
    for q in range(2):
        columns = pl.ds(pl.multiple_of(q * RH + c * RQ, RQ), RQ)
        b_copies.append(pltpu.make_async_copy(basis_ref.at[:, columns], bfull.at[q, yh, x, z], lsem.at[5 + q]))
        b_copies[q].start()
    barrier = pltpu.get_barrier_semaphore()
    peers = [other_core, mirror]
    peers += [comm.dev(x=wrap(x + j, NX)) for j in range(1, NX)]
    peers += [comm.dev(z=wrap(z + k, NZ)) for k in (1, -1, 2, -2)]
    peers += [comm.dev(yl=wrap(yl + r, NY)) for r in range(1, NY)]
    for peer in peers:
        pl.semaphore_signal(barrier, inc=1, device_id=peer, device_id_type=MESH)

    row0 = pl.multiple_of(yh * BLK, BLK)
    tok_copy = pltpu.make_async_copy(tok_ref, toks.at[c], lsem.at[0])
    up_copy = pltpu.make_async_copy(up_ref, upv, lsem.at[1])
    m_copy = pltpu.make_async_copy(m_ref, mom.at[0, pl.ds(row0, BLK)], lsem.at[2])
    v_copy = pltpu.make_async_copy(v_ref, mom.at[1, pl.ds(row0, BLK)], lsem.at[3])
    bas_copy = pltpu.make_async_copy(basis_ref, bas, lsem.at[4])
    for copy in b_copies:
        copy.wait()
    pl.semaphore_wait(barrier, len(peers))

    def send_mirror(q):
        comm.send("mirror", q, bfull.at[q, yh, x, z], bfull.at[q, yh, x, z], mirror)

    def recv_mirror(q):
        comm.wait("mirror", q)

    def load_rest():
        for copy in (up_copy, m_copy, v_copy, bas_copy):
            copy.start()

    def send_tokens():
        tok_copy.start()
        comm.send("tok", 0, tok_ref, toks.at[c], other_core)

    def recv_tokens():
        tok_copy.wait()
        comm.wait("tok", 0)

    def send_moments():
        comm.send("moments", 0, m_ref, mom.at[0, pl.ds(row0, BLK)], other_run)
        comm.send("moments", 0, v_ref, mom.at[1, pl.ds(row0, BLK)], other_run)

    def project(q):
        proj = jnp.zeros((2 * TOK, RQ), jnp.float32)
        depth = NZ * BROWS
        for a in range(2):
            for b in range(NX):
                left = toks[:, :, pl.ds((a * NX + b) * depth, depth)].reshape(2 * TOK, depth)
                proj += jnp.dot(left, bfull[q, a, b].reshape(depth, RQ), preferred_element_type=jnp.float32)
        piece = pall.at[q, c, yl]
        piece[...] = proj.astype(jnp.bfloat16)
        for r in (2, 1, 3):
            comm.send("p", (q, r % 2), piece, piece, comm.dev(yl=wrap(yl + r, NY)))
        comm.send("core", q, piece, piece, other_core)

    def collect(q):
        for r in (1, 3, 2):
            piece = pall.at[q, c, wrap(yl - r, NY)]
            if r != 3:
                comm.wait("p", (q, r % 2))
            comm.send("core", q, piece, piece, other_core)

    def product(q):
        comm.wait("core", q)
        for half in range(2):
            pt[half] = pall[q, half].reshape(NY * 2 * TOK, RQ).T

        def tile(i, carry):
            columns = pl.ds(pl.multiple_of(i * 256, 256), 256)
            left = pt[...].reshape(RH, NY * 2 * TOK)
            grad[q, :, columns] = jnp.dot(left, upv[:, columns], preferred_element_type=jnp.float32)
            return carry

        lax.fori_loop(0, FFL // 256, tile, 0)

    def block_of(q):
        def block(half, xo, zo):
            rows = pl.ds(pl.multiple_of((xo * NZ + zo) * BLK, BLK), BLK)
            start, width = (WA, WB // 2) if half else (0, WA // 2)
            parts = [grad[q, rows, pl.ds(start + i * width, width)] for i in range(2)]
            return jnp.concatenate(parts, axis=0)

        return block

    scatters = [
        Scatter(
            comm, ("rs", q), block_of(q),
            *(ref.at[q] for ref in (sa, ra, sb, rb, asum, sax, rax, sbz, rbz)),
        )
        for q in range(2)
    ]
    sums = [[None, None], [None, None]]

    def finish_half(q, half):
        value = scatters[q].last_b((0,)) if half else scatters[q].total_a()
        ys, yr = ((ysa, yra), (ysb, yrb))[half]
        ys[q] = value.astype(jnp.bfloat16)
        comm.send("y", (q, half), ys.at[q], yr.at[q], other_run)
        sums[q][half] = value

    def exchange(q):
        rows = pl.ds(q * BLK, BLK)
        for half, (yr, start, width) in enumerate(((yra, 0, WA // 2), (yrb, WA, WB // 2))):
            comm.wait("y", (q, half))
            value = (sums[q][half] + yr[q].astype(jnp.float32)) * (1.0 / (NY * 2 * TOK * 64))
            for i in range(2):
                gsum[rows, pl.ds(start + i * width, width)] = value[i * BLK:(i + 1) * BLK]

    tasks = [(2.0, send_tokens), (6.0, load_rest), (15.9, recv_tokens), (22.9, up_copy.wait), (32.0, send_moments)]
    for q, late in ((0, 0.0), (1, 6.5)):
        tasks += [
            (0.3 * late, functools.partial(send_mirror, q)),
            (late + 4.4, functools.partial(recv_mirror, q)),
        ]
        tasks += gather(
            comm, ("basis", q),
            lambda xo, zo, q=q: bfull.at[q, yh, xo, zo],
            lambda xo, zo, q=q: bfull.at[q, 1 - yh, xo, zo],
            late, late + 4.5,
        )
        tasks += [
            (late + 16.0, functools.partial(project, q)),
            (late + 21.5, functools.partial(collect, q)),
            (late + 23.0, functools.partial(product, q)),
        ]
        tasks += scatters[q].steps(late + 24.5)
        tasks += [
            (late + 38.0, functools.partial(finish_half, q, 1)),
            (late + 34.8, functools.partial(finish_half, q, 0)),
            (late + 43.0, functools.partial(exchange, q)),
        ]
    run(tasks)
    g = gsum[...]

    sq = jnp.sum(g * g, axis=0, keepdims=True)
    part = sq[:, 0:128]
    for i in range(1, FFL // 128):
        part = part + sq[:, i * 128:(i + 1) * 128]
    n1[0] = part
    for j in range(NX):
        for k in range(NZ):
            if j or k:
                comm.send(
                    "n1", 0, n1.at[0], n1.at[j * NZ + k],
                    comm.dev(x=wrap(x + j, NX), z=wrap(z + k, NZ)),
                )
    comm.wait("n1", 0, n1.at[pl.ds(1, NX * NZ - 1)])
    n2[0] = jnp.sum(n1[...], axis=0)
    for r in range(NY):
        for e in range(2):
            if r or e:
                comm.send(
                    "n2", 0, n2.at[0], n2.at[r * 2 + e],
                    comm.dev(yl=wrap(yl + r, NY), c=lax.rem(c + e, 2)),
                )
    bas_copy.wait()
    row = lax.broadcasted_iota(jnp.int32, (R, R), 0)
    column = lax.broadcasted_iota(jnp.int32, (R, R), 1)
    source = ((column >> 3) & 1) * RH + (column >> 4) * BLK + (column & 7)
    pick = jnp.where(row == source, 1.0, 0.0).astype(jnp.bfloat16)
    bp[...] = jnp.dot(bas[...], pick, preferred_element_type=jnp.float32).astype(jnp.bfloat16)
    m_copy.wait()
    v_copy.wait()
    comm.wait("moments", 0)
    comm.wait("n2", 0, n2.at[pl.ds(1, NY * 2 - 1)])
    norm = jnp.sqrt(jnp.sum(jnp.sum(n2[...], axis=0), axis=1, keepdims=True))
    clipped = g * jnp.minimum(1.0, 1.0 / norm)
    new_first = 0.9 * mom[0] + 0.1 * clipped
    new_second = 0.999 * mom[1] + 0.001 * clipped * clipped
    first_fix = 1.0 - 0.9**20
    second_fix = 1.0 - 0.999**20
    direction = (new_first / first_fix / (jnp.sqrt(new_second / second_fix) + 1e-08)).astype(jnp.bfloat16)
    da[x, z] = direction[:, :DA]
    db[x, z] = direction[:, DA:]

    run(gather(comm, "direction", lambda xo, zo: da.at[xo, zo], lambda xo, zo: db.at[xo, zo], 0.0, 0.0))
    for start, full, width in ((0, da, DA), (DA, db, DB)):
        out_ref[:, pl.ds(start, width)] = jnp.dot(
            bp[...], full[...].reshape(R, width), preferred_element_type=jnp.float32
        )
    comm.sent("n1", n1.at[pl.ds(1, NX * NZ - 1)])
    comm.sent("n2", n2.at[pl.ds(1, NY * 2 - 1)])
    comm.finish()


N_PHASES, N_GROUPS = 18, 70


def local(tokens, up_cotangent, basis, first_moment, second_moment):
    bf, f32 = jnp.bfloat16, jnp.float32
    hbm_spec = pl.BlockSpec(memory_space=pltpu.HBM)
    vmem_spec = pl.BlockSpec(memory_space=pltpu.VMEM)
    return pl.pallas_call(
        kernel,
        out_shape=jax.ShapeDtypeStruct((BROWS, FFL), f32),
        in_specs=[hbm_spec] * 5,
        out_specs=vmem_spec,
        scratch_shapes=[
            pltpu.VMEM((2, TOK, 4096), bf),
            pltpu.VMEM((NY * 2 * TOK, FFL), bf),
            pltpu.VMEM((BROWS, R), bf),
            pltpu.VMEM((2, 2, NX, NZ, BROWS, RQ), bf),
            pltpu.VMEM((2, 2, NY, 2 * TOK, RQ), bf),
            pltpu.VMEM((2, RQ, NY * 2 * TOK), bf),
            pltpu.VMEM((2, RH, FFL), f32),
            pltpu.VMEM((2, 2 * BLK, FFL), f32),
            pltpu.VMEM((BROWS, R), bf),
            pltpu.VMEM((2, NZ, NX, 16, WA // 2), bf),
            pltpu.VMEM((2, NZ, NX, 16, WA // 2), bf),
            pltpu.VMEM((2, 2, 2, NZ, 16, WB // 2), bf),
            pltpu.VMEM((2, 2, 2, NZ, 16, WB // 2), bf),
            pltpu.VMEM((2, NX, 16, WA // 2), f32),
            pltpu.VMEM((2, NX, 16, WA // 2), bf),
            pltpu.VMEM((2, NX, 16, WA // 2), bf),
            pltpu.VMEM((2, NZ, 16, WB // 2), bf),
            pltpu.VMEM((2, NZ, 16, WB // 2), bf),
            pltpu.VMEM((2, 16, WA // 2), bf),
            pltpu.VMEM((2, 16, WA // 2), bf),
            pltpu.VMEM((2, 16, WB // 2), bf),
            pltpu.VMEM((2, 16, WB // 2), bf),
            pltpu.VMEM((2 * BLK, FFL), f32),
            pltpu.VMEM((NX * NZ, 1, 128), f32),
            pltpu.VMEM((NY * 2, 1, 128), f32),
            pltpu.VMEM((NX, NZ, 16, DA), bf),
            pltpu.VMEM((NX, NZ, 16, DB), bf),
            pltpu.VMEM((UNITS, 16, 128), bf),
            pltpu.SemaphoreType.DMA((7,)),
            pltpu.SemaphoreType.DMA((N_PHASES,)),
            pltpu.SemaphoreType.DMA((N_GROUPS,)),
        ],
        compiler_params=pltpu.CompilerParams(
            collective_id=0, has_side_effects=True, vmem_limit_bytes=63 * 2**20
        ),
        cost_estimate=pl.CostEstimate(flops=4 * 10**9, bytes_accessed=2 * 10**7, transcendentals=0),
        name="galore_step",
    )(tokens, up_cotangent, basis, first_moment, second_moment)


def solution(mesh):
    in_specs = (
        P(("dp", "tensor"), None),
        P("dp", "tensor"),
        P("dp", None),
        P("dp", "tensor"),
        P("dp", "tensor"),
    )
    out_specs = P("dp", "tensor")
    return jax.shard_map(local, mesh=mesh, in_specs=in_specs, out_specs=out_specs, check_vma=False)
```

```python
import functools

import jax
import jax.numpy as jnp
from jax import lax
from jax.experimental import pallas as pl
from jax.experimental.pallas import tpu as pltpu
from jax.sharding import PartitionSpec as P

MESH = pl.DeviceIdType.MESH
NX, NZ, NY = 4, 8, 4
BLK = 8
TOK = 96
FFL = 1792
WA, WB = 512, 1280
DA, DB = 640, 1152
R = 512
RH = R // 2
RQ = RH // 2
BROWS = 64
X_ORDER = (0, 1, 3, 2)
Z_ORDER = (0, 1, -1, 2, -2, 3, -3, 4)
SIDES = (1, -1)


UNIT = 16 * 128 * 2
UNITS = 320


class Comm:
    def __init__(self, ssem, rsem, tally, coords):
        self.ssem, self.rsem, self.tally, self.coords = ssem, rsem, tally, coords
        self.groups, self.phases, self.coming, self.going = {}, {}, {}, {}

    def dev(self, yh=None, x=None, z=None, yl=None, c=None):
        own = self.coords
        yh, x, z, yl, c = (o if v is None else v for v, o in zip((yh, x, z, yl, c), own))
        return (yh * 32 + x * 8 + z, yl * 2 + c)

    def send(self, phase, group, src, dst, dev):
        i = self.phases.setdefault(phase, len(self.phases))
        j = self.groups.setdefault((phase, group), len(self.groups))
        pltpu.make_async_remote_copy(
            src_ref=src, dst_ref=dst, send_sem=self.ssem.at[i], recv_sem=self.rsem.at[j],
            device_id=dev, device_id_type=MESH,
        ).start()
        size = src.dtype.itemsize
        for n in src.shape:
            size *= n
        self.going[phase] = self.going.get(phase, 0) + size
        self.coming[phase, group] = self.coming.get((phase, group), 0) + size

    def total(self, size, ref):
        if ref is None:
            assert size % UNIT == 0 and size <= UNIT * UNITS
            ref = self.tally.at[pl.ds(0, size // UNIT)]
        return ref

    def wait(self, phase, group, ref=None):
        ref = self.total(self.coming.pop((phase, group)), ref)
        j = self.groups[phase, group]
        pltpu.make_async_remote_copy(
            src_ref=ref, dst_ref=ref, send_sem=self.ssem.at[0], recv_sem=self.rsem.at[j],
            device_id=self.dev(), device_id_type=MESH,
        ).wait_recv()

    def sent(self, phase, ref=None):
        ref = self.total(self.going.pop(phase), ref)
        pltpu.make_async_remote_copy(
            src_ref=ref, dst_ref=ref, send_sem=self.ssem.at[self.phases[phase]], recv_sem=self.rsem.at[0],
            device_id=self.dev(), device_id_type=MESH,
        ).wait_send()

    def finish(self):
        for phase in list(self.going):
            self.sent(phase)


def wrap(v, n):
    return lax.rem(v + n, n)


def run(tasks):
    for _, step in sorted(tasks, key=lambda task: task[0]):
        step()


def gather(comm, name, view_a, view_b, begin, begin_b):
    _, x, z, _, c = comm.coords
    turn = 1 - 2 * c

    def zs(k):
        return wrap(z + turn * k, NZ)

    near = {0: 0, 1: 1, 3: 1, 2: 2}
    far = {0: 0, 1: 1, -1: 1, 2: 2, -2: 2, 3: 3, -3: 3, 4: 3}
    name_a, name_b = (name, "a"), (name, "b")

    def send_ax():
        for j in X_ORDER[1:]:
            comm.send(name_a, ("x", near[j]), view_a(x, z), view_a(x, z), comm.dev(x=wrap(x + j, NX)))

    def pass_a(xo, origin, hop, group):
        comm.send(name_a, group, view_a(xo, origin), view_a(xo, origin), comm.dev(z=zs(hop)))

    def near_a(js):
        if js[0]:
            comm.wait(name_a, ("x", near[js[0]]))
        for j in js:
            xo = wrap(x - j, NX)
            for hop in (2, -2, 1, -1):
                pass_a(xo, z, hop, ("z", near[j]) if hop in (2, -2) else "z")

    def far_a(js):
        comm.wait(name_a, ("z", near[js[0]]))
        for j in js:
            xo = wrap(x - j, NX)
            pass_a(xo, zs(-2), 2, "z")
            pass_a(xo, zs(-2), 1, "z")
            pass_a(xo, zs(2), -1, "z")

    def last_a():
        comm.wait(name_a, "z")

    def send_b(k, origin, hop):
        comm.send(name_b, ("z", far[k]), view_b(x, origin), view_b(x, origin), comm.dev(z=zs(hop)))

    def send_bz():
        for k in (2, -2, 1, -1):
            send_b(k, z, k)

    def cross_b(ks):
        if ks[0]:
            comm.wait(name_b, ("z", far[ks[0]]))
        for k in ks:
            zo = zs(-k)
            if k == 2:
                send_b(4, zo, 2)
                send_b(3, zo, 1)
            if k == -2:
                send_b(-3, zo, -1)
        for k in ks:
            zo = zs(-k)
            for j in X_ORDER[1:]:
                comm.send(name_b, "x", view_b(x, zo), view_b(x, zo), comm.dev(x=wrap(x + j, NX)))

    def last_b():
        comm.wait(name_b, "x")

    steps_a = [
        (0.0, send_ax), (0.0, lambda: near_a((0,))), (2.8, lambda: near_a((1, 3))), (3.3, lambda: far_a((0,))),
        (3.4, lambda: near_a((2,))), (6.2, lambda: far_a((1, 3))), (6.9, lambda: far_a((2,))), (11.0, last_a),
    ]
    steps_b = [
        (0.0, send_bz), (0.0, lambda: cross_b((0,))), (3.3, lambda: cross_b((2, -2))), (3.4, lambda: cross_b((1, -1))),
        (6.8, lambda: cross_b((4, 3, -3))), (11.0, last_b),
    ]
    return [(begin + t, f) for t, f in steps_a] + [(begin_b + t, f) for t, f in steps_b]


class Scatter:
    def __init__(self, comm, name, block, sa, ra, sb, rb, asum, sax, rax, sbz, rbz):
        self.comm, self.name_a, self.name_b, self.block = comm, (name, "a"), (name, "b"), block
        self.last = {0: 0, 1: 1, -1: 1, 2: 2, -2: 2, 3: 3, -3: 3, 4: 3}
        self.sa, self.ra, self.sb, self.rb = sa, ra, sb, rb
        self.asum, self.sax, self.rax, self.sbz, self.rbz = asum, sax, rax, sbz, rbz
        _, self.x, self.z, _, c = comm.coords
        self.turn = 1 - 2 * c

    def zs(self, k):
        return wrap(self.z + self.turn * k, NZ)

    def pass_a(self, j, k, hop, others, group):
        value = self.block(0, j, self.zs(k))
        for other in others:
            value = value + self.ra[other % NZ, j].astype(jnp.float32)
        out = self.sa.at[k % NZ, j]
        out[...] = value.astype(jnp.bfloat16)
        self.comm.send(self.name_a, group, out, self.ra.at[k % NZ, j], self.comm.dev(z=self.zs(hop)))

    def far_a(self, part):
        for j in (2 * part, 2 * part + 1):
            self.pass_a(j, 4, 2, (), ("far", part))
            self.pass_a(j, 3, 1, (), ("far", part))
            self.pass_a(j, -3, -1, (), ("far", part))

    def near_a(self, part):
        for j in (2 * part, 2 * part + 1):
            self.pass_a(j, 1, 1, (), "near")
            self.pass_a(j, -1, -1, (), "near")

    def mid_a(self, part):
        self.comm.wait(self.name_a, ("far", part))
        for j in (2 * part, 2 * part + 1):
            self.pass_a(j, 2, 2, (3, 4), "near")
            self.pass_a(j, -2, -2, (-3,), "near")

    def cross_b(self, ks):
        for k in ks:
            for j in (2, 1, 3):
                xo = wrap(self.x + j, NX)
                out = self.sb.at[j, k % NZ]
                out[...] = self.block(1, xo, self.zs(k)).astype(jnp.bfloat16)
                self.comm.send(self.name_b, (1, self.last[k]), out, self.rb.at[j, k % NZ], self.comm.dev(x=xo))

    def last_a(self):
        comm = self.comm
        comm.wait(self.name_a, "near")
        for j in range(NX):
            value = self.block(0, j, self.z)
            for k in (1, -1, 2, -2):
                value = value + self.ra[k % NZ, j].astype(jnp.float32)
            self.asum[j] = value
            self.sax[j] = value.astype(jnp.bfloat16)
        for j in (2, 1, 3):
            xo = wrap(self.x + j, NX)
            comm.send(self.name_a, "x", self.sax.at[xo], self.rax.at[j], comm.dev(x=xo))

    def total_a(self):
        value = self.asum[self.x]
        self.comm.wait(self.name_a, "x")
        for j in (1, 3, 2):
            value = value + self.rax[j].astype(jnp.float32)
        return value

    def last_b(self, ks):
        comm = self.comm
        hop = {3: 1, -3: -1, 4: 2}
        plus = {2: (3, 4), -2: (-3,), 0: (1, -1, 2, -2)}
        comm.wait(self.name_b, (1, self.last[ks[0]]))
        if ks[0] in (0, 2):
            comm.wait(self.name_b, ("z", ks[0]))
        for k in ks:
            value = self.block(1, self.x, self.zs(k))
            for j in (1, 2, 3):
                value = value + self.rb[j, k % NZ].astype(jnp.float32)
            for other in plus.get(k, ()):
                value = value + self.rbz[other % NZ].astype(jnp.float32)
            if k == 0:
                return value
            self.sbz[k % NZ] = value.astype(jnp.bfloat16)
            comm.send(
                self.name_b, ("z", 2 if k in hop else 0), self.sbz.at[k % NZ], self.rbz.at[k % NZ],
                comm.dev(z=self.zs(hop.get(k, k))),
            )

    def steps(self, begin):
        steps = [
            (0.0, lambda: self.cross_b((4, 3, -3))), (0.1, lambda: self.far_a(0)), (0.2, lambda: self.far_a(1)),
            (0.3, lambda: self.cross_b((1, -1))), (0.4, lambda: self.near_a(0)), (0.5, lambda: self.cross_b((2, -2))),
            (0.6, lambda: self.near_a(1)), (0.7, lambda: self.cross_b((0,))),
            (3.4, lambda: self.mid_a(0)), (3.6, lambda: self.mid_a(1)), (4.0, lambda: self.last_b((4, 3, -3))),
            (5.5, lambda: self.last_b((1, -1))), (7.2, self.last_a), (7.3, lambda: self.last_b((2, -2))),
        ]
        return [(begin + t, f) for t, f in steps]


def kernel(
    tok_ref, up_ref, basis_ref, m_ref, v_ref, out_ref,
    toks, upv, bas, bfull, pall, pt, grad, mom, bp,
    sa, ra, sb, rb, asum, sax, rax, sbz, rbz, ysa, yra, ysb, yrb, gsum, n1, n2, da, db,
    tally, lsem, ssem, rsem,
):
    d, t = lax.axis_index("dp"), lax.axis_index("tensor")
    yh, x, z, yl, c = lax.div(d, 32), lax.rem(lax.div(d, 8), 4), lax.rem(d, 8), lax.div(t, 2), lax.rem(t, 2)
    comm = Comm(ssem, rsem, tally, (yh, x, z, yl, c))
    other_core = comm.dev(c=1 - c)
    other_run = comm.dev(yh=1 - yh)
    mirror = comm.dev(yh=1 - yh, yl=3 - yl)

    b_copies = []
    for q in range(2):
        columns = pl.ds(pl.multiple_of(q * RH + c * RQ, RQ), RQ)
        b_copies.append(pltpu.make_async_copy(basis_ref.at[:, columns], bfull.at[q, yh, x, z], lsem.at[5 + q]))
        b_copies[q].start()
    barrier = pltpu.get_barrier_semaphore()
    peers = [other_core, mirror]
    peers += [comm.dev(x=wrap(x + j, NX)) for j in range(1, NX)]
    peers += [comm.dev(z=wrap(z + k, NZ)) for k in (1, -1, 2, -2)]
    peers += [comm.dev(yl=wrap(yl + r, NY)) for r in range(1, NY)]
    for peer in peers:
        pl.semaphore_signal(barrier, inc=1, device_id=peer, device_id_type=MESH)

    row0 = pl.multiple_of(yh * BLK, BLK)
    tok_copy = pltpu.make_async_copy(tok_ref, toks.at[c], lsem.at[0])
    up_copy = pltpu.make_async_copy(up_ref, upv, lsem.at[1])
    m_copy = pltpu.make_async_copy(m_ref, mom.at[0, pl.ds(row0, BLK)], lsem.at[2])
    v_copy = pltpu.make_async_copy(v_ref, mom.at[1, pl.ds(row0, BLK)], lsem.at[3])
    bas_copy = pltpu.make_async_copy(basis_ref, bas, lsem.at[4])
    for copy in b_copies:
        copy.wait()
    pl.semaphore_wait(barrier, len(peers))

    def send_mirror(q):
        comm.send("mirror", q, bfull.at[q, yh, x, z], bfull.at[q, yh, x, z], mirror)

    def recv_mirror(q):
        comm.wait("mirror", q)

    def load_rest():
        for copy in (up_copy, m_copy, v_copy, bas_copy):
            copy.start()

    def send_tokens():
        tok_copy.start()
        comm.send("tok", 0, tok_ref, toks.at[c], other_core)

    def recv_tokens():
        tok_copy.wait()
        comm.wait("tok", 0)

    def send_moments():
        comm.send("moments", 0, m_ref, mom.at[0, pl.ds(row0, BLK)], other_run)
        comm.send("moments", 0, v_ref, mom.at[1, pl.ds(row0, BLK)], other_run)

    def project(q):
        proj = jnp.zeros((2 * TOK, RQ), jnp.float32)
        depth = NZ * BROWS
        for a in range(2):
            for b in range(NX):
                left = toks[:, :, pl.ds((a * NX + b) * depth, depth)].reshape(2 * TOK, depth)
                proj += jnp.dot(left, bfull[q, a, b].reshape(depth, RQ), preferred_element_type=jnp.float32)
        piece = pall.at[q, c, yl]
        piece[...] = proj.astype(jnp.bfloat16)
        for r in (2, 1, 3):
            comm.send("p", (q, r % 2), piece, piece, comm.dev(yl=wrap(yl + r, NY)))
        comm.send("core", q, piece, piece, other_core)

    def collect(q):
        for r in (1, 3, 2):
            piece = pall.at[q, c, wrap(yl - r, NY)]
            if r != 3:
                comm.wait("p", (q, r % 2))
            comm.send("core", q, piece, piece, other_core)

    def product(q):
        comm.wait("core", q)
        for half in range(2):
            pt[half] = pall[q, half].reshape(NY * 2 * TOK, RQ).T

        def tile(i, carry):
            columns = pl.ds(pl.multiple_of(i * 256, 256), 256)
            left = pt[...].reshape(RH, NY * 2 * TOK)
            grad[q, :, columns] = jnp.dot(left, upv[:, columns], preferred_element_type=jnp.float32)
            return carry

        lax.fori_loop(0, FFL // 256, tile, 0)

    def block_of(q):
        def block(half, xo, zo):
            rows = pl.ds(pl.multiple_of((xo * NZ + zo) * BLK, BLK), BLK)
            start, width = (WA, WB // 2) if half else (0, WA // 2)
            parts = [grad[q, rows, pl.ds(start + i * width, width)] for i in range(2)]
            return jnp.concatenate(parts, axis=0)

        return block

    scatters = [
        Scatter(
            comm, ("rs", q), block_of(q),
            *(ref.at[q] for ref in (sa, ra, sb, rb, asum, sax, rax, sbz, rbz)),
        )
        for q in range(2)
    ]
    sums = [[None, None], [None, None]]

    def finish_half(q, half):
        value = scatters[q].last_b((0,)) if half else scatters[q].total_a()
        ys, yr = ((ysa, yra), (ysb, yrb))[half]
        ys[q] = value.astype(jnp.bfloat16)
        comm.send("y", (q, half), ys.at[q], yr.at[q], other_run)
        sums[q][half] = value

    def exchange(q):
        rows = pl.ds(q * BLK, BLK)
        for half, (yr, start, width) in enumerate(((yra, 0, WA // 2), (yrb, WA, WB // 2))):
            comm.wait("y", (q, half))
            value = (sums[q][half] + yr[q].astype(jnp.float32)) * (1.0 / (NY * 2 * TOK * 64))
            for i in range(2):
                gsum[rows, pl.ds(start + i * width, width)] = value[i * BLK:(i + 1) * BLK]

    tasks = [(2.0, send_tokens), (6.0, load_rest), (15.9, recv_tokens), (22.9, up_copy.wait), (32.0, send_moments)]
    for q, late in ((0, 0.0), (1, 6.5)):
        tasks += [
            (0.3 * late, functools.partial(send_mirror, q)),
            (late + 4.4, functools.partial(recv_mirror, q)),
        ]
        tasks += gather(
            comm, ("basis", q),
            lambda xo, zo, q=q: bfull.at[q, yh, xo, zo],
            lambda xo, zo, q=q: bfull.at[q, 1 - yh, xo, zo],
            late, late + 4.5,
        )
        tasks += [
            (late + 16.0, functools.partial(project, q)),
            (late + 21.5, functools.partial(collect, q)),
            (late + 23.0, functools.partial(product, q)),
        ]
        tasks += scatters[q].steps(late + 24.5)
        tasks += [
            (late + 35.6, functools.partial(finish_half, q, 1)),
            (late + 34.8, functools.partial(finish_half, q, 0)),
            (late + 40.5, functools.partial(exchange, q)),
        ]
    run(tasks)
    g = gsum[...]

    sq = jnp.sum(g * g, axis=0, keepdims=True)
    part = sq[:, 0:128]
    for i in range(1, FFL // 128):
        part = part + sq[:, i * 128:(i + 1) * 128]
    n1[0] = part
    for j in range(NX):
        for k in range(NZ):
            if j or k:
                comm.send(
                    "n1", 0, n1.at[0], n1.at[j * NZ + k],
                    comm.dev(x=wrap(x + j, NX), z=wrap(z + k, NZ)),
                )
    comm.wait("n1", 0, n1.at[pl.ds(1, NX * NZ - 1)])
    n2[0] = jnp.sum(n1[...], axis=0)
    for r in range(NY):
        for e in range(2):
            if r or e:
                comm.send(
                    "n2", 0, n2.at[0], n2.at[r * 2 + e],
                    comm.dev(yl=wrap(yl + r, NY), c=lax.rem(c + e, 2)),
                )
    bas_copy.wait()
    row = lax.broadcasted_iota(jnp.int32, (R, R), 0)
    column = lax.broadcasted_iota(jnp.int32, (R, R), 1)
    source = ((column >> 3) & 1) * RH + (column >> 4) * BLK + (column & 7)
    pick = jnp.where(row == source, 1.0, 0.0).astype(jnp.bfloat16)
    bp[...] = jnp.dot(bas[...], pick, preferred_element_type=jnp.float32).astype(jnp.bfloat16)
    m_copy.wait()
    v_copy.wait()
    comm.wait("moments", 0)
    comm.wait("n2", 0, n2.at[pl.ds(1, NY * 2 - 1)])
    norm = jnp.sqrt(jnp.sum(jnp.sum(n2[...], axis=0), axis=1, keepdims=True))
    clipped = g * jnp.minimum(1.0, 1.0 / norm)
    new_first = 0.9 * mom[0] + 0.1 * clipped
    new_second = 0.999 * mom[1] + 0.001 * clipped * clipped
    first_fix = 1.0 - 0.9**20
    second_fix = 1.0 - 0.999**20
    direction = (new_first / first_fix / (jnp.sqrt(new_second / second_fix) + 1e-08)).astype(jnp.bfloat16)
    da[x, z] = direction[:, :DA]
    db[x, z] = direction[:, DA:]

    run(gather(comm, "direction", lambda xo, zo: da.at[xo, zo], lambda xo, zo: db.at[xo, zo], 0.0, 0.0))
    for start, full, width in ((0, da, DA), (DA, db, DB)):
        out_ref[:, pl.ds(start, width)] = jnp.dot(
            bp[...], full[...].reshape(R, width), preferred_element_type=jnp.float32
        )
    comm.sent("n1", n1.at[pl.ds(1, NX * NZ - 1)])
    comm.sent("n2", n2.at[pl.ds(1, NY * 2 - 1)])
    comm.finish()


N_PHASES, N_GROUPS = 18, 66


def local(tokens, up_cotangent, basis, first_moment, second_moment):
    bf, f32 = jnp.bfloat16, jnp.float32
    hbm_spec = pl.BlockSpec(memory_space=pltpu.HBM)
    vmem_spec = pl.BlockSpec(memory_space=pltpu.VMEM)
    return pl.pallas_call(
        kernel,
        out_shape=jax.ShapeDtypeStruct((BROWS, FFL), f32),
        in_specs=[hbm_spec] * 5,
        out_specs=vmem_spec,
        scratch_shapes=[
            pltpu.VMEM((2, TOK, 4096), bf),
            pltpu.VMEM((NY * 2 * TOK, FFL), bf),
            pltpu.VMEM((BROWS, R), bf),
            pltpu.VMEM((2, 2, NX, NZ, BROWS, RQ), bf),
            pltpu.VMEM((2, 2, NY, 2 * TOK, RQ), bf),
            pltpu.VMEM((2, RQ, NY * 2 * TOK), bf),
            pltpu.VMEM((2, RH, FFL), f32),
            pltpu.VMEM((2, 2 * BLK, FFL), f32),
            pltpu.VMEM((BROWS, R), bf),
            pltpu.VMEM((2, NZ, NX, 16, WA // 2), bf),
            pltpu.VMEM((2, NZ, NX, 16, WA // 2), bf),
            pltpu.VMEM((2, NX, NZ, 16, WB // 2), bf),
            pltpu.VMEM((2, NX, NZ, 16, WB // 2), bf),
            pltpu.VMEM((2, NX, 16, WA // 2), f32),
            pltpu.VMEM((2, NX, 16, WA // 2), bf),
            pltpu.VMEM((2, NX, 16, WA // 2), bf),
            pltpu.VMEM((2, NZ, 16, WB // 2), bf),
            pltpu.VMEM((2, NZ, 16, WB // 2), bf),
            pltpu.VMEM((2, 16, WA // 2), bf),
            pltpu.VMEM((2, 16, WA // 2), bf),
            pltpu.VMEM((2, 16, WB // 2), bf),
            pltpu.VMEM((2, 16, WB // 2), bf),
            pltpu.VMEM((2 * BLK, FFL), f32),
            pltpu.VMEM((NX * NZ, 1, 128), f32),
            pltpu.VMEM((NY * 2, 1, 128), f32),
            pltpu.VMEM((NX, NZ, 16, DA), bf),
            pltpu.VMEM((NX, NZ, 16, DB), bf),
            pltpu.VMEM((UNITS, 16, 128), bf),
            pltpu.SemaphoreType.DMA((7,)),
            pltpu.SemaphoreType.DMA((N_PHASES,)),
            pltpu.SemaphoreType.DMA((N_GROUPS,)),
        ],
        compiler_params=pltpu.CompilerParams(
            collective_id=0, has_side_effects=True, vmem_limit_bytes=63 * 2**20
        ),
        cost_estimate=pl.CostEstimate(flops=4 * 10**9, bytes_accessed=2 * 10**7, transcendentals=0),
        name="galore_step",
    )(tokens, up_cotangent, basis, first_moment, second_moment)


def solution(mesh):
    in_specs = (
        P(("dp", "tensor"), None),
        P("dp", "tensor"),
        P("dp", None),
        P("dp", "tensor"),
        P("dp", "tensor"),
    )
    out_specs = P("dp", "tensor")
    return jax.shard_map(local, mesh=mesh, in_specs=in_specs, out_specs=out_specs, check_vma=False)
```

```python
import functools

import jax
import jax.numpy as jnp
from jax import lax
from jax.experimental import pallas as pl
from jax.experimental.pallas import tpu as pltpu
from jax.sharding import PartitionSpec as P

MESH = pl.DeviceIdType.MESH
NX, NZ, NY = 4, 8, 4
BLK = 8
TOK = 96
FFL = 1792
WA, WB = 768, 1024
DA, DB = 640, 1152
R = 512
RH = R // 2
RQ = RH // 2
BROWS = 64
X_ORDER = (0, 1, 3, 2)
Z_ORDER = (0, 1, -1, 2, -2, 3, -3, 4)
SIDES = (1, -1)


UNIT = 16 * 128 * 2
UNITS = 320


class Comm:
    def __init__(self, ssem, rsem, tally, coords):
        self.ssem, self.rsem, self.tally, self.coords = ssem, rsem, tally, coords
        self.groups, self.phases, self.coming, self.going = {}, {}, {}, {}

    def dev(self, yh=None, x=None, z=None, yl=None, c=None):
        own = self.coords
        yh, x, z, yl, c = (o if v is None else v for v, o in zip((yh, x, z, yl, c), own))
        return (yh * 32 + x * 8 + z, yl * 2 + c)

    def send(self, phase, group, src, dst, dev):
        i = self.phases.setdefault(phase, len(self.phases))
        j = self.groups.setdefault((phase, group), len(self.groups))
        pltpu.make_async_remote_copy(
            src_ref=src, dst_ref=dst, send_sem=self.ssem.at[i], recv_sem=self.rsem.at[j],
            device_id=dev, device_id_type=MESH,
        ).start()
        size = src.dtype.itemsize
        for n in src.shape:
            size *= n
        self.going[phase] = self.going.get(phase, 0) + size
        self.coming[phase, group] = self.coming.get((phase, group), 0) + size

    def total(self, size, ref):
        if ref is None:
            assert size % UNIT == 0 and size <= UNIT * UNITS
            ref = self.tally.at[pl.ds(0, size // UNIT)]
        return ref

    def wait(self, phase, group, ref=None):
        ref = self.total(self.coming.pop((phase, group)), ref)
        j = self.groups[phase, group]
        pltpu.make_async_remote_copy(
            src_ref=ref, dst_ref=ref, send_sem=self.ssem.at[0], recv_sem=self.rsem.at[j],
            device_id=self.dev(), device_id_type=MESH,
        ).wait_recv()

    def sent(self, phase, ref=None):
        ref = self.total(self.going.pop(phase), ref)
        pltpu.make_async_remote_copy(
            src_ref=ref, dst_ref=ref, send_sem=self.ssem.at[self.phases[phase]], recv_sem=self.rsem.at[0],
            device_id=self.dev(), device_id_type=MESH,
        ).wait_send()

    def finish(self):
        for phase in list(self.going):
            self.sent(phase)


def wrap(v, n):
    return lax.rem(v + n, n)


def run(tasks):
    for _, step in sorted(tasks, key=lambda task: task[0]):
        step()


def gather(comm, name, view_a, view_b, begin, begin_b):
    _, x, z, _, c = comm.coords
    turn = 1 - 2 * c

    def zs(k):
        return wrap(z + turn * k, NZ)

    near = {0: 0, 1: 1, 3: 1, 2: 2}
    far = {0: 0, 1: 1, -1: 1, 2: 2, -2: 2, 3: 3, -3: 3, 4: 3}
    name_a, name_b = (name, "a"), (name, "b")

    def send_ax():
        for j in X_ORDER[1:]:
            comm.send(name_a, ("x", near[j]), view_a(x, z), view_a(x, z), comm.dev(x=wrap(x + j, NX)))

    def pass_a(xo, origin, hop, group):
        comm.send(name_a, group, view_a(xo, origin), view_a(xo, origin), comm.dev(z=zs(hop)))

    def near_a(js):
        if js[0]:
            comm.wait(name_a, ("x", near[js[0]]))
        for j in js:
            xo = wrap(x - j, NX)
            for hop in (2, -2, 1, -1):
                pass_a(xo, z, hop, ("z", near[j]) if hop in (2, -2) else "z")

    def far_a(js):
        comm.wait(name_a, ("z", near[js[0]]))
        for j in js:
            xo = wrap(x - j, NX)
            pass_a(xo, zs(-2), 2, "z")
            pass_a(xo, zs(-2), 1, "z")
            pass_a(xo, zs(2), -1, "z")

    def last_a():
        comm.wait(name_a, "z")

    def send_b(k, origin, hop):
        comm.send(name_b, ("z", far[k]), view_b(x, origin), view_b(x, origin), comm.dev(z=zs(hop)))

    def send_bz():
        for k in (2, -2, 1, -1):
            send_b(k, z, k)

    def cross_b(ks):
        if ks[0]:
            comm.wait(name_b, ("z", far[ks[0]]))
        for k in ks:
            zo = zs(-k)
            if k == 2:
                send_b(4, zo, 2)
                send_b(3, zo, 1)
            if k == -2:
                send_b(-3, zo, -1)
        for k in ks:
            zo = zs(-k)
            for j in X_ORDER[1:]:
                comm.send(name_b, "x", view_b(x, zo), view_b(x, zo), comm.dev(x=wrap(x + j, NX)))

    def last_b():
        comm.wait(name_b, "x")

    steps_a = [
        (0.0, send_ax), (0.0, lambda: near_a((0,))), (2.8, lambda: near_a((1, 3))), (3.3, lambda: far_a((0,))),
        (3.4, lambda: near_a((2,))), (6.2, lambda: far_a((1, 3))), (6.9, lambda: far_a((2,))), (11.0, last_a),
    ]
    steps_b = [
        (0.0, send_bz), (0.0, lambda: cross_b((0,))), (3.3, lambda: cross_b((2, -2))), (3.4, lambda: cross_b((1, -1))),
        (6.8, lambda: cross_b((4, 3, -3))), (11.0, last_b),
    ]
    return [(begin + t, f) for t, f in steps_a] + [(begin_b + t, f) for t, f in steps_b]


class Scatter:
    def __init__(self, comm, name, block, sa, ra, sb, rb, asum, sax, rax, sbz, rbz):
        self.comm, self.name_a, self.name_b, self.block = comm, (name, "a"), (name, "b"), block
        self.last = {0: 0, 1: 1, -1: 1, 2: 2, -2: 2, 3: 3, -3: 3, 4: 3}
        self.sa, self.ra, self.sb, self.rb = sa, ra, sb, rb
        self.asum, self.sax, self.rax, self.sbz, self.rbz = asum, sax, rax, sbz, rbz
        _, self.x, self.z, _, c = comm.coords
        self.turn = 1 - 2 * c

    def zs(self, k):
        return wrap(self.z + self.turn * k, NZ)

    def pass_a(self, j, k, hop, others, group):
        value = self.block(0, j, self.zs(k))
        for other in others:
            value = value + self.ra[other % NZ, j].astype(jnp.float32)
        out = self.sa.at[k % NZ, j]
        out[...] = value.astype(jnp.bfloat16)
        self.comm.send(self.name_a, group, out, self.ra.at[k % NZ, j], self.comm.dev(z=self.zs(hop)))

    def far_a(self, part):
        for j in (2 * part, 2 * part + 1):
            self.pass_a(j, 4, 2, (), ("far", part))
            self.pass_a(j, 3, 1, (), ("far", part))
            self.pass_a(j, -3, -1, (), ("far", part))

    def near_a(self, part):
        for j in (2 * part, 2 * part + 1):
            self.pass_a(j, 1, 1, (), "near")
            self.pass_a(j, -1, -1, (), "near")

    def mid_a(self, part):
        self.comm.wait(self.name_a, ("far", part))
        for j in (2 * part, 2 * part + 1):
            self.pass_a(j, 2, 2, (3, 4), "near")
            self.pass_a(j, -2, -2, (-3,), "near")

    def cross_b(self, ks):
        for k in ks:
            for j in (2, 1, 3):
                xo = wrap(self.x + j, NX)
                out = self.sb.at[j, k % NZ]
                out[...] = self.block(1, xo, self.zs(k)).astype(jnp.bfloat16)
                self.comm.send(self.name_b, (1, self.last[k]), out, self.rb.at[j, k % NZ], self.comm.dev(x=xo))

    def last_a(self):
        comm = self.comm
        comm.wait(self.name_a, "near")
        for j in range(NX):
            value = self.block(0, j, self.z)
            for k in (1, -1, 2, -2):
                value = value + self.ra[k % NZ, j].astype(jnp.float32)
            self.asum[j] = value
            self.sax[j] = value.astype(jnp.bfloat16)
        for j in (2, 1, 3):
            xo = wrap(self.x + j, NX)
            comm.send(self.name_a, "x", self.sax.at[xo], self.rax.at[j], comm.dev(x=xo))

    def total_a(self):
        value = self.asum[self.x]
        self.comm.wait(self.name_a, "x")
        for j in (1, 3, 2):
            value = value + self.rax[j].astype(jnp.float32)
        return value

    def last_b(self, ks):
        comm = self.comm
        hop = {3: 1, -3: -1, 4: 2}
        plus = {2: (3, 4), -2: (-3,), 0: (1, -1, 2, -2)}
        comm.wait(self.name_b, (1, self.last[ks[0]]))
        if ks[0] in (0, 2):
            comm.wait(self.name_b, ("z", ks[0]))
        for k in ks:
            value = self.block(1, self.x, self.zs(k))
            for j in (1, 2, 3):
                value = value + self.rb[j, k % NZ].astype(jnp.float32)
            for other in plus.get(k, ()):
                value = value + self.rbz[other % NZ].astype(jnp.float32)
            if k == 0:
                return value
            self.sbz[k % NZ] = value.astype(jnp.bfloat16)
            comm.send(
                self.name_b, ("z", 2 if k in hop else 0), self.sbz.at[k % NZ], self.rbz.at[k % NZ],
                comm.dev(z=self.zs(hop.get(k, k))),
            )

    def steps(self, begin):
        steps = [
            (0.0, lambda: self.cross_b((4, 3, -3))), (0.1, lambda: self.far_a(0)), (0.2, lambda: self.far_a(1)),
            (0.3, lambda: self.cross_b((1, -1))), (0.4, lambda: self.near_a(0)), (0.5, lambda: self.cross_b((2, -2))),
            (0.6, lambda: self.near_a(1)), (0.7, lambda: self.cross_b((0,))),
            (3.4, lambda: self.mid_a(0)), (3.6, lambda: self.mid_a(1)), (4.0, lambda: self.last_b((4, 3, -3))),
            (5.5, lambda: self.last_b((1, -1))), (7.2, self.last_a), (7.3, lambda: self.last_b((2, -2))),
        ]
        return [(begin + t, f) for t, f in steps]


def kernel(
    tok_ref, up_ref, basis_ref, m_ref, v_ref, out_ref,
    toks, upv, bas, bfull, pall, pt, grad, mom, bp,
    sa, ra, sb, rb, asum, sax, rax, sbz, rbz, ysa, yra, ysb, yrb, gsum, n1, n2, da, db,
    tally, lsem, ssem, rsem,
):
    d, t = lax.axis_index("dp"), lax.axis_index("tensor")
    yh, x, z, yl, c = lax.div(d, 32), lax.rem(lax.div(d, 8), 4), lax.rem(d, 8), lax.div(t, 2), lax.rem(t, 2)
    comm = Comm(ssem, rsem, tally, (yh, x, z, yl, c))
    other_core = comm.dev(c=1 - c)
    other_run = comm.dev(yh=1 - yh)
    mirror = comm.dev(yh=1 - yh, yl=3 - yl)

    b_copies = []
    for q in range(2):
        columns = pl.ds(pl.multiple_of(q * RH + c * RQ, RQ), RQ)
        b_copies.append(pltpu.make_async_copy(basis_ref.at[:, columns], bfull.at[q, yh, x, z], lsem.at[5 + q]))
        b_copies[q].start()
    barrier = pltpu.get_barrier_semaphore()
    peers = [other_core, mirror]
    peers += [comm.dev(x=wrap(x + j, NX)) for j in range(1, NX)]
    peers += [comm.dev(z=wrap(z + k, NZ)) for k in (1, -1, 2, -2)]
    peers += [comm.dev(yl=wrap(yl + r, NY)) for r in range(1, NY)]
    for peer in peers:
        pl.semaphore_signal(barrier, inc=1, device_id=peer, device_id_type=MESH)

    row0 = pl.multiple_of(yh * BLK, BLK)
    tok_copy = pltpu.make_async_copy(tok_ref, toks.at[c], lsem.at[0])
    up_copy = pltpu.make_async_copy(up_ref, upv, lsem.at[1])
    m_copy = pltpu.make_async_copy(m_ref, mom.at[0, pl.ds(row0, BLK)], lsem.at[2])
    v_copy = pltpu.make_async_copy(v_ref, mom.at[1, pl.ds(row0, BLK)], lsem.at[3])
    bas_copy = pltpu.make_async_copy(basis_ref, bas, lsem.at[4])
    for copy in b_copies:
        copy.wait()
    pl.semaphore_wait(barrier, len(peers))

    def send_mirror(q):
        comm.send("mirror", q, bfull.at[q, yh, x, z], bfull.at[q, yh, x, z], mirror)

    def recv_mirror(q):
        comm.wait("mirror", q)

    def load_rest():
        for copy in (up_copy, m_copy, v_copy, bas_copy):
            copy.start()

    def send_tokens():
        tok_copy.start()
        comm.send("tok", 0, tok_ref, toks.at[c], other_core)

    def recv_tokens():
        tok_copy.wait()
        comm.wait("tok", 0)

    def send_moments():
        comm.send("moments", 0, m_ref, mom.at[0, pl.ds(row0, BLK)], other_run)
        comm.send("moments", 0, v_ref, mom.at[1, pl.ds(row0, BLK)], other_run)

    def project(q):
        proj = jnp.zeros((2 * TOK, RQ), jnp.float32)
        depth = NZ * BROWS
        for a in range(2):
            for b in range(NX):
                left = toks[:, :, pl.ds((a * NX + b) * depth, depth)].reshape(2 * TOK, depth)
                proj += jnp.dot(left, bfull[q, a, b].reshape(depth, RQ), preferred_element_type=jnp.float32)
        piece = pall.at[q, c, yl]
        piece[...] = proj.astype(jnp.bfloat16)
        for r in (2, 1, 3):
            comm.send("p", (q, r % 2), piece, piece, comm.dev(yl=wrap(yl + r, NY)))
        comm.send("core", q, piece, piece, other_core)

    def collect(q):
        for r in (1, 3, 2):
            piece = pall.at[q, c, wrap(yl - r, NY)]
            if r != 3:
                comm.wait("p", (q, r % 2))
            comm.send("core", q, piece, piece, other_core)

    def product(q):
        comm.wait("core", q)
        for half in range(2):
            pt[half] = pall[q, half].reshape(NY * 2 * TOK, RQ).T

        def tile(i, carry):
            columns = pl.ds(pl.multiple_of(i * 256, 256), 256)
            left = pt[...].reshape(RH, NY * 2 * TOK)
            grad[q, :, columns] = jnp.dot(left, upv[:, columns], preferred_element_type=jnp.float32)
            return carry

        lax.fori_loop(0, FFL // 256, tile, 0)

    def block_of(q):
        def block(half, xo, zo):
            rows = pl.ds(pl.multiple_of((xo * NZ + zo) * BLK, BLK), BLK)
            start, width = (WA, WB // 2) if half else (0, WA // 2)
            parts = [grad[q, rows, pl.ds(start + i * width, width)] for i in range(2)]
            return jnp.concatenate(parts, axis=0)

        return block

    scatters = [
        Scatter(
            comm, ("rs", q), block_of(q),
            *(ref.at[q] for ref in (sa, ra, sb, rb, asum, sax, rax, sbz, rbz)),
        )
        for q in range(2)
    ]
    sums = [[None, None], [None, None]]

    def finish_half(q, half):
        value = scatters[q].last_b((0,)) if half else scatters[q].total_a()
        ys, yr = ((ysa, yra), (ysb, yrb))[half]
        ys[q] = value.astype(jnp.bfloat16)
        comm.send("y", (q, half), ys.at[q], yr.at[q], other_run)
        sums[q][half] = value

    def exchange(q):
        rows = pl.ds(q * BLK, BLK)
        for half, (yr, start, width) in enumerate(((yra, 0, WA // 2), (yrb, WA, WB // 2))):
            comm.wait("y", (q, half))
            value = (sums[q][half] + yr[q].astype(jnp.float32)) * (1.0 / (NY * 2 * TOK * 64))
            for i in range(2):
                gsum[rows, pl.ds(start + i * width, width)] = value[i * BLK:(i + 1) * BLK]

    tasks = [(2.0, send_tokens), (6.0, load_rest), (15.9, recv_tokens), (22.9, up_copy.wait), (32.0, send_moments)]
    for q, late in ((0, 0.0), (1, 6.5)):
        tasks += [
            (0.3 * late, functools.partial(send_mirror, q)),
            (late + 4.4, functools.partial(recv_mirror, q)),
        ]
        tasks += gather(
            comm, ("basis", q),
            lambda xo, zo, q=q: bfull.at[q, yh, xo, zo],
            lambda xo, zo, q=q: bfull.at[q, 1 - yh, xo, zo],
            late, late + 4.5,
        )
        tasks += [
            (late + 16.0, functools.partial(project, q)),
            (late + 21.5, functools.partial(collect, q)),
            (late + 23.0, functools.partial(product, q)),
        ]
        tasks += scatters[q].steps(late + 24.5)
        tasks += [
            (late + 35.6, functools.partial(finish_half, q, 1)),
            (late + 34.8, functools.partial(finish_half, q, 0)),
            (late + 40.5, functools.partial(exchange, q)),
        ]
    run(tasks)
    g = gsum[...]

    sq = jnp.sum(g * g, axis=0, keepdims=True)
    part = sq[:, 0:128]
    for i in range(1, FFL // 128):
        part = part + sq[:, i * 128:(i + 1) * 128]
    n1[0] = part
    for j in range(NX):
        for k in range(NZ):
            if j or k:
                comm.send(
                    "n1", 0, n1.at[0], n1.at[j * NZ + k],
                    comm.dev(x=wrap(x + j, NX), z=wrap(z + k, NZ)),
                )
    comm.wait("n1", 0, n1.at[pl.ds(1, NX * NZ - 1)])
    n2[0] = jnp.sum(n1[...], axis=0)
    for r in range(NY):
        for e in range(2):
            if r or e:
                comm.send(
                    "n2", 0, n2.at[0], n2.at[r * 2 + e],
                    comm.dev(yl=wrap(yl + r, NY), c=lax.rem(c + e, 2)),
                )
    bas_copy.wait()
    row = lax.broadcasted_iota(jnp.int32, (R, R), 0)
    column = lax.broadcasted_iota(jnp.int32, (R, R), 1)
    source = ((column >> 3) & 1) * RH + (column >> 4) * BLK + (column & 7)
    pick = jnp.where(row == source, 1.0, 0.0).astype(jnp.bfloat16)
    bp[...] = jnp.dot(bas[...], pick, preferred_element_type=jnp.float32).astype(jnp.bfloat16)
    m_copy.wait()
    v_copy.wait()
    comm.wait("moments", 0)
    comm.wait("n2", 0, n2.at[pl.ds(1, NY * 2 - 1)])
    norm = jnp.sqrt(jnp.sum(jnp.sum(n2[...], axis=0), axis=1, keepdims=True))
    clipped = g * jnp.minimum(1.0, 1.0 / norm)
    new_first = 0.9 * mom[0] + 0.1 * clipped
    new_second = 0.999 * mom[1] + 0.001 * clipped * clipped
    first_fix = 1.0 - 0.9**20
    second_fix = 1.0 - 0.999**20
    direction = (new_first / first_fix / (jnp.sqrt(new_second / second_fix) + 1e-08)).astype(jnp.bfloat16)
    da[x, z] = direction[:, :DA]
    db[x, z] = direction[:, DA:]

    run(gather(comm, "direction", lambda xo, zo: da.at[xo, zo], lambda xo, zo: db.at[xo, zo], 0.0, 0.0))
    for start, full, width in ((0, da, DA), (DA, db, DB)):
        out_ref[:, pl.ds(start, width)] = jnp.dot(
            bp[...], full[...].reshape(R, width), preferred_element_type=jnp.float32
        )
    comm.sent("n1", n1.at[pl.ds(1, NX * NZ - 1)])
    comm.sent("n2", n2.at[pl.ds(1, NY * 2 - 1)])
    comm.finish()


N_PHASES, N_GROUPS = 18, 66


def local(tokens, up_cotangent, basis, first_moment, second_moment):
    bf, f32 = jnp.bfloat16, jnp.float32
    hbm_spec = pl.BlockSpec(memory_space=pltpu.HBM)
    vmem_spec = pl.BlockSpec(memory_space=pltpu.VMEM)
    return pl.pallas_call(
        kernel,
        out_shape=jax.ShapeDtypeStruct((BROWS, FFL), f32),
        in_specs=[hbm_spec] * 5,
        out_specs=vmem_spec,
        scratch_shapes=[
            pltpu.VMEM((2, TOK, 4096), bf),
            pltpu.VMEM((NY * 2 * TOK, FFL), bf),
            pltpu.VMEM((BROWS, R), bf),
            pltpu.VMEM((2, 2, NX, NZ, BROWS, RQ), bf),
            pltpu.VMEM((2, 2, NY, 2 * TOK, RQ), bf),
            pltpu.VMEM((2, RQ, NY * 2 * TOK), bf),
            pltpu.VMEM((2, RH, FFL), f32),
            pltpu.VMEM((2, 2 * BLK, FFL), f32),
            pltpu.VMEM((BROWS, R), bf),
            pltpu.VMEM((2, NZ, NX, 16, WA // 2), bf),
            pltpu.VMEM((2, NZ, NX, 16, WA // 2), bf),
            pltpu.VMEM((2, NX, NZ, 16, WB // 2), bf),
            pltpu.VMEM((2, NX, NZ, 16, WB // 2), bf),
            pltpu.VMEM((2, NX, 16, WA // 2), f32),
            pltpu.VMEM((2, NX, 16, WA // 2), bf),
            pltpu.VMEM((2, NX, 16, WA // 2), bf),
            pltpu.VMEM((2, NZ, 16, WB // 2), bf),
            pltpu.VMEM((2, NZ, 16, WB // 2), bf),
            pltpu.VMEM((2, 16, WA // 2), bf),
            pltpu.VMEM((2, 16, WA // 2), bf),
            pltpu.VMEM((2, 16, WB // 2), bf),
            pltpu.VMEM((2, 16, WB // 2), bf),
            pltpu.VMEM((2 * BLK, FFL), f32),
            pltpu.VMEM((NX * NZ, 1, 128), f32),
            pltpu.VMEM((NY * 2, 1, 128), f32),
            pltpu.VMEM((NX, NZ, 16, DA), bf),
            pltpu.VMEM((NX, NZ, 16, DB), bf),
            pltpu.VMEM((UNITS, 16, 128), bf),
            pltpu.SemaphoreType.DMA((7,)),
            pltpu.SemaphoreType.DMA((N_PHASES,)),
            pltpu.SemaphoreType.DMA((N_GROUPS,)),
        ],
        compiler_params=pltpu.CompilerParams(
            collective_id=0, has_side_effects=True, vmem_limit_bytes=63 * 2**20
        ),
        cost_estimate=pl.CostEstimate(flops=4 * 10**9, bytes_accessed=2 * 10**7, transcendentals=0),
        name="galore_step",
    )(tokens, up_cotangent, basis, first_moment, second_moment)


def solution(mesh):
    in_specs = (
        P(("dp", "tensor"), None),
        P("dp", "tensor"),
        P("dp", None),
        P("dp", "tensor"),
        P("dp", "tensor"),
    )
    out_specs = P("dp", "tensor")
    return jax.shard_map(local, mesh=mesh, in_specs=in_specs, out_specs=out_specs, check_vma=False)
```
